512 devices in a mesh: row: 64 (over z, x, y_hi), rep: 8 (over y_lo, core).
Axes of the slice: x: 4, y: 8 (y_hi: 2, y_lo: 4; y = y_hi * 4 + y_lo), z: 8, core: 2. Of those that a mesh axis runs over, the one named last changes fastest.
Arguments:
- out_grad: bfloat16 [131072, 256], P(('rep', 'row')), may hold values from -6 to 6
- node_input: bfloat16 [131072, 256], P(('row', 'rep')), may hold values from -0.015625 to 0.015625
- weight: bfloat16 [256, 256], replicated, may hold values from -0.375 to 0.375
- tile_vals: bfloat16 [64, 8, 128, 128, 128], P('row', 'rep'), may hold values from -0.25 to 0.25
- tile_rows: int32 [64, 8, 128], P('row', 'rep'), may hold values from 0 to 15, as said below
- tile_cols: int32 [64, 8, 128], P('row', 'rep'), may hold values from 0 to 127
- tile_count: int32 [64, 8], P('row', 'rep'), may hold values from 32 to 128, as said below
Outputs:
- input_grad: bfloat16 [131072, 256], P(('row', 'rep'))
- weight_grad: float32 [256, 256], replicated
The draws below stay inside these ranges and needn't reach their ends.
Inputs may be any that keep to these rules, and one draw needn't show every extreme that they name: On one device no pair (tile_rows, tile_cols) repeats among all 128 list entries. `tile_count`: entries at or past a device's count are padding. Some device has exactly 128 live entries in every draw.
All inputs are finite; a program needn't handle non-finite values.
Results may differ from the reference program's by a relative error of at most 0.005.
Values may be sent and summed in bfloat16 or wider, within the bound.
A program may use at most 64 MiB of HBM per device.

```python
import jax
import jax.numpy as jnp
from jax import lax

F = 256
TILE = 128
SLABS = 64
GROUPS = 8
SLAB_TILES = 16
GROUP_TILES = 128
NODES = 131072
MAX_TILES = 128


def tile_pairs(key):
    key = jax.random.fold_in(key, 7)
    device_keys = jax.random.split(key, SLABS * GROUPS)

    def one_device(device_key):
        return jax.random.permutation(device_key, SLAB_TILES * GROUP_TILES)[:MAX_TILES]
    picked = jax.vmap(one_device)(device_keys)
    return picked.reshape(SLABS, GROUPS, MAX_TILES).astype(jnp.int32)


def draw_tile_rows(key, part):
    return (tile_pairs(key) // GROUP_TILES).astype(jnp.int32)


def draw_tile_cols(key, part):
    return (tile_pairs(key) % GROUP_TILES).astype(jnp.int32)


def draw_tile_count(key, part):
    key = jax.random.fold_in(key, 3)
    first_key, second_key = jax.random.split(key)
    live_counts = jax.random.randint(first_key, (SLABS * GROUPS,), MAX_TILES // 4, MAX_TILES // 2 + 1, dtype=jnp.int32)
    busiest = jax.random.randint(second_key, (), 0, SLABS * GROUPS, dtype=jnp.int32)
    device_ids = jnp.arange(SLABS * GROUPS, dtype=jnp.int32)
    flattened = jnp.where(device_ids == busiest, jnp.int32(MAX_TILES), live_counts)
    return flattened.reshape(SLABS, GROUPS).astype(jnp.int32)


def block_scale(rng, shape, cuts, smallest, top_value):
    factor_of = 1.0
    for dim, blocks in cuts:
        heights = jax.random.uniform(jax.random.fold_in(jax.random.fold_in(rng, 6), dim), (blocks,), jnp.float32, smallest / len(cuts), top_value / len(cuts))
        factor_of = factor_of * jnp.repeat(jnp.exp(heights), shape[dim] // blocks).reshape((-1,) + (1,) * (len(shape) - 1 - dim))
    return factor_of


def normal_values(key, extent, deviation, reach, shards=(), kind=jnp.bfloat16):
    values = jax.random.normal(key, extent, jnp.float32) * deviation
    if len(shards) > 0:
        values = block_scale(key, extent, shards, -0.22, 0.18) * values
    return jnp.clip(values, min=-reach, max=reach).astype(kind)


def setup_inputs(seed: int = 0) -> dict:
    key_of = jax.random.split(jax.random.key(seed), 8)
    out_grad = normal_values(key_of[0], (NODES, F), 1.0, 6.0, ((0, 512),))
    node_input = normal_values(key_of[1], (NODES, F), (1.0 / NODES ** 0.5), 0.015625, ((0, 512),))
    weight = normal_values(key_of[2], (F, F), F ** -0.5, 0.375)
    tile_vals = normal_values(key_of[3], (SLABS, GROUPS, MAX_TILES, TILE, TILE), (TILE * 4) ** -0.5, 0.25, ((0, 64), (1, 8)))
    tile_rows = draw_tile_rows(jax.random.fold_in(key_of[7], 71), 0)
    tile_cols = draw_tile_cols(jax.random.fold_in(key_of[7], 71), 0)
    tile_count = draw_tile_count(jax.random.fold_in(key_of[7], 71), 0)
    return {"out_grad": out_grad, "node_input": node_input, "weight": weight, "tile_vals": tile_vals, "tile_rows": tile_rows, "tile_cols": tile_cols, "tile_count": tile_count}


def slab_product(out_grad, tile_vals, tile_rows, tile_cols, tile_count, slab_index):
    by_group = out_grad.reshape(GROUPS, GROUP_TILES, TILE, F)
    slab_ids = jnp.arange(SLAB_TILES, dtype=jnp.int32)
    entry_ids = jnp.arange(MAX_TILES, dtype=jnp.int32)

    def group_term(group_index):
        blocks = jnp.take(by_group[group_index], tile_cols[slab_index, group_index], axis=0).astype(jnp.float32)
        values = tile_vals[slab_index, group_index].astype(jnp.float32)
        product = jnp.einsum('tij,tjf->tif', values, blocks, precision=lax.Precision.HIGHEST)
        live_mask = (entry_ids < tile_count[slab_index, group_index]).astype(jnp.float32)
        selector = (tile_rows[slab_index, group_index][:, None] == slab_ids[None, :]).astype(jnp.float32)
        selector = selector * live_mask[:, None]
        return jnp.einsum('ts,tif->sif', selector, product, precision=lax.Precision.HIGHEST)

    return jnp.sum(lax.map(group_term, jnp.arange(GROUPS, dtype=jnp.int32)), axis=0)


def reference(out_grad, node_input, weight, tile_vals, tile_rows, tile_cols, tile_count):
    def one_slab(slab_index):
        return slab_product(out_grad, tile_vals, tile_rows, tile_cols, tile_count, slab_index)

    node_grad = lax.map(one_slab, jnp.arange(SLABS, dtype=jnp.int32)).reshape(NODES, F)
    node_grad_b = node_grad.astype(jnp.bfloat16)
    input_grad = jnp.dot(node_grad_b, weight.T, preferred_element_type=jnp.float32).astype(jnp.bfloat16)
    weight_grad = jnp.dot(node_input.astype(jnp.float32).T, node_grad, precision=lax.Precision.HIGHEST)
    return input_grad, weight_grad
```

```python
import heapq

import jax
import jax.numpy as jnp
from jax import lax
from jax.experimental import pallas as pl
from jax.experimental.pallas import tpu as pltpu
from jax.sharding import PartitionSpec as P

MESH = pl.DeviceIdType.MESH
Z, X, YH, YL, CORES = 8, 4, 2, 4, 2
PLANE = Z * X
Y = YH * YL
TILE = 128
CAP = 128
F = 256
ROWS = 256
UNIT = 16
UNITS = ROWS // UNIT
FIRST = (96, 112)


def gather_edges():
    edges = []

    def chain(rnd, part, axis, base, tie):
        half = (Z if axis == 0 else X) // 2

        def at(k):
            return (base[0] + k, base[1]) if axis == 0 else (base[0], base[1] + k)

        for k in range(1, half + (tie > 0)):
            edges.append((rnd, part, at(k - 1), at(k), axis, 1))
        for k in range(1, half + (tie < 0)):
            edges.append((rnd, part, at(1 - k), at(-k), axis, -1))

    for rnd in (0, 1):
        tie = 1 if rnd == 0 else -1
        chain(rnd, 0, 1, (0, 0), tie)
        for dx in (-1, 0, 1, 2 * tie):
            chain(rnd, 0, 0, (0, dx), 1 if dx in (0, 1) else -1)
        chain(rnd, 1, 0, (0, 0), tie)
        for dz in (-3, -2, -1, 0, 1, 2, 3, 4 * tie):
            chain(rnd, 1, 1, (dz, 0), 1 if 0 <= dz <= 3 else -1)
    return edges


def part_rows(rnd, part):
    return (0, FIRST[rnd]) if part == 0 else (FIRST[rnd], ROWS - FIRST[rnd])


def gather_order(edges):
    kids = {}
    for i, (rnd, part, frm, to, axis, way) in enumerate(edges):
        kids.setdefault((rnd, part, frm), []).append(i)

    def size(i):
        rnd, part, _, to, _, _ = edges[i]
        return 1 + sum(size(j) for j in kids.get((rnd, part, to), []))

    queue = [(0.0, 0, (0, 0, (0, 0)), -1), (0.0, 1, (0, 1, (0, 0)), -1)]
    queue += [(11.0, 2, (1, 0, (0, 0)), -1), (11.0, 3, (1, 1, (0, 0)), -1)]
    free, count, order = {}, 4, []
    while queue:
        now, _, node, via = heapq.heappop(queue)
        starts = sorted(kids.get(node, []), key=lambda i: -size(i))
        order.append((node, via, starts))
        for i in starts:
            rnd, part, _, to, axis, way = edges[i]
            begin = max(now, free.get((axis, way), 0.0))
            end = begin + part_rows(rnd, part)[1] * 0.01024
            free[(axis, way)] = end
            heapq.heappush(queue, (end + 1.0, count, (rnd, part, to), i))
            count += 1
    return order


EDGES = gather_edges()
ORDER = gather_order(EDGES)


def schedule(rows_ref, cols_ref, count_ref, meta_ref):
    lane = lax.broadcasted_iota(jnp.int32, (TILE, TILE), 1)
    sub = lax.broadcasted_iota(jnp.int32, (TILE, TILE), 0)

    def wide(value):
        return jnp.broadcast_to(value, (TILE, TILE))

    live = lane < wide(count_ref[...])
    row = jnp.where(live, wide(rows_ref[...]), 16)
    key = row * CAP + lane
    row_t, key_t, col_t = row.T, key.T, wide(cols_ref[...]).T

    def total(value):
        return jnp.sum(value, axis=0, keepdims=True)

    rank = total((key_t < key).astype(jnp.int32))
    match = wide(rank).T == lane
    order = total(jnp.where(match, sub, 0))
    col = total(jnp.where(match, col_t, 0))
    sorted_row = total(jnp.where(match, row_t, 0))
    first = total((row_t < sorted_row).astype(jnp.int32)) == lane[:1]
    upto = total((row_t <= lane).astype(jnp.int32))
    has = total((row_t == lane).astype(jnp.int32))
    slot = jnp.where(has > 0, upto, 0)
    meta_ref[0:1, :] = order
    meta_ref[1:2, :] = col
    meta_ref[2:3, :] = jnp.where(first, 0, lane[:1])
    meta_ref[3:4, :] = slot
    meta_ref[4:8, :] = jnp.zeros((4, TILE), jnp.int32)


def kernel(
    grad_ref, node_ref, weight_ref, vals_ref, meta_s,
    dx_ref, dw_ref,
    grads, tiles, sums, high, low, nodes, nodes_t, sib, outgoing, incoming,
    w_part, w_sib, w_half, w_plane, w_unit, w_y, w_full,
    local_sem, gs_sem, gr_sem, ys_sem, yr_sem, ns_sem, nr_sem, ss_sem, sr_sem,
    rs_sem, rr_sem, w0_sem, p1s_sem, p1r_sem, us_sem, ur_sem, p2s_sem, p2r_sem, w4_sem,
):
    me = lax.axis_index("row")
    rep = lax.axis_index("rep")
    z, x, yh = me // (X * YH), (me // YH) % X, me % YH
    yl, core = rep // CORES, rep % CORES
    y = yh * YL + yl
    u = z * X + x
    sibling = (me, rep + 1 - 2 * core)

    def plane_peer(k):
        return ((u + k) % PLANE * YH + yh, rep)

    def y_peer(k):
        other = (y + k) % Y
        return (u * YH + other // YL, other % YL * CORES + core)

    def rep_peer(k):
        return (me, (yl + k) % YL * CORES + core)

    own_copies = [
        pltpu.make_async_copy(grad_ref, grads.at[pl.ds(me * UNITS, UNITS)], local_sem.at[0]),
        pltpu.make_async_copy(node_ref, nodes.at[rep], local_sem.at[1]),
        pltpu.make_async_copy(vals_ref, tiles, local_sem.at[2]),
    ]
    for copy in own_copies:
        copy.start()

    barrier = pltpu.get_barrier_semaphore()

    def greet(k, carry):
        pl.semaphore_signal(barrier, inc=1, device_id=plane_peer(k), device_id_type=MESH)
        return carry

    lax.fori_loop(1, PLANE, greet, 0)
    for k in range(1, Y):
        pl.semaphore_signal(barrier, inc=1, device_id=y_peer(k), device_id_type=MESH)
    pl.semaphore_signal(barrier, inc=1, device_id=sibling, device_id_type=MESH)
    pl.semaphore_wait(barrier, PLANE - 1 + Y - 1 + 1)

    def piece(rnd, part, offset):
        pz, px = (z - offset[0] + Z) % Z, (x - offset[1] + X) % X
        py = yh if rnd == 0 else 1 - yh
        begin, size = part_rows(rnd, part)
        return grads.at[pl.ds(((pz * X + px) * YH + py) * UNITS + begin // UNIT, size // UNIT)]

    def hop(i, landed):
        rnd, part, frm, to, axis, way = EDGES[i]
        ref = piece(rnd, part, to if landed else frm)
        nz = (z + way + Z) % Z if axis == 0 else z
        nx = (x + way + X) % X if axis == 1 else x
        return pltpu.make_async_remote_copy(
            src_ref=ref, dst_ref=ref, send_sem=gs_sem.at[i], recv_sem=gr_sem.at[i],
            device_id=((nz * X + nx) * YH + yh, rep), device_id_type=MESH,
        )

    own_copies[0].wait()
    partner = ((u * YH) + 1 - yh, rep)

    def across(index):
        ref = grads.at[pl.ds((u * YH + index) * UNITS, UNITS)]
        return pltpu.make_async_remote_copy(
            src_ref=ref, dst_ref=ref, send_sem=ys_sem.at[0], recv_sem=yr_sem.at[0],
            device_id=partner, device_id_type=MESH,
        )

    sent = []
    for step, (node, via, starts) in enumerate(ORDER):
        if not starts:
            continue
        if via >= 0:
            hop(via, True).wait_recv()
        elif node == (1, 0, (0, 0)):
            across(1 - yh).wait_recv()
        for i in starts:
            copy = hop(i, False)
            copy.start()
            sent.append(copy)
        if step == 1:
            across_copy = across(yh)
            across_copy.start()
            own_copies[1].wait()

            def node_copy(k, landed):
                block = nodes.at[rep_peer(YL - k)[1] if landed else rep]
                return pltpu.make_async_remote_copy(
                    src_ref=block, dst_ref=block, send_sem=ns_sem.at[k], recv_sem=nr_sem.at[k],
                    device_id=rep_peer(k), device_id_type=MESH,
                )

            def node_pass(k, landed):
                source = rep_peer(YL - k)[1]
                block = nodes.at[source + 1 - 2 * core if landed else source]
                return pltpu.make_async_remote_copy(
                    src_ref=block, dst_ref=block, send_sem=ns_sem.at[YL + k], recv_sem=nr_sem.at[YL + k],
                    device_id=sibling, device_id_type=MESH,
                )

            node_sent = [node_copy(k, False) for k in range(1, YL)] + [node_pass(0, False)]
            for copy in node_sent:
                copy.start()
            sums[0] = jnp.zeros((TILE, F), jnp.float32)

    for k in range(1, YL):
        node_copy(k, True).wait_recv()
        copy = node_pass(k, False)
        copy.start()
        node_sent.append(copy)
    for k in range(YL):
        node_pass(k, True).wait_recv()
    for q in range(YL * CORES):
        nodes_t[:, q * ROWS:(q + 1) * ROWS] = nodes[q].T
    own_copies[2].wait()
    for node, via, starts in ORDER:
        if not starts:
            hop(via, True).wait_recv()

    def tile_step(i, carry):
        unit = meta_s[1, i] * (TILE // UNIT)
        block = jnp.concatenate([grads[unit + j] for j in range(TILE // UNIT)], axis=0)
        product = jnp.dot(tiles[meta_s[0, i]], block, preferred_element_type=jnp.float32)
        sums[i + 1] = sums[meta_s[2, i]] + product
        return carry

    lax.fori_loop(0, CAP, tile_step, 0, unroll=8)

    def take_sum(s, carry):
        total = sums[meta_s[3, s]]
        top = total.astype(jnp.bfloat16)
        at = pl.ds(pl.multiple_of(s * TILE, TILE), TILE)
        high[at] = top
        low[at] = (total - top.astype(jnp.float32)).astype(jnp.bfloat16)
        return carry

    lax.fori_loop(0, 16, take_sum, 0, unroll=2)

    def block_of(index):
        return pl.ds(pl.multiple_of(index * ROWS, ROWS), ROWS)

    def sib_copy(k):
        dest = (yl + k) % YL
        return pltpu.make_async_remote_copy(
            src_ref=high.at[block_of(dest * CORES + 1 - core)], dst_ref=sib.at[dest],
            send_sem=ss_sem.at[k], recv_sem=sr_sem.at[k], device_id=sibling, device_id_type=MESH,
        )

    sib_sent = [sib_copy(k) for k in (2, 1, 3, 0)]
    for copy in sib_sent:
        copy.start()

    def w_dot(half):
        left = nodes_t[pl.ds(pl.multiple_of(half * TILE, TILE), TILE)]
        term = jnp.dot(left, high[...], preferred_element_type=jnp.float32)
        term += jnp.dot(left, low[...], preferred_element_type=jnp.float32)
        for h in range(2):
            w_part[half, h * 16:(h + 1) * 16] = term[:, h * TILE:(h + 1) * TILE].reshape(16, 8, TILE)

    w_dot(1 - core)
    w_copy = pltpu.make_async_remote_copy(
        src_ref=w_part.at[1 - core], dst_ref=w_sib, send_sem=w0_sem.at[0], recv_sem=w0_sem.at[1],
        device_id=sibling, device_id_type=MESH,
    )
    w_copy.start()
    w_dot(core)

    def both(index, at):
        rows = block_of(index)
        return high[rows].astype(jnp.float32) + low[rows].astype(jnp.float32) + sib[at].astype(jnp.float32)

    def out_copy(k):
        return pltpu.make_async_remote_copy(
            src_ref=outgoing.at[k], dst_ref=incoming.at[k], send_sem=rs_sem.at[k], recv_sem=rr_sem.at[k],
            device_id=rep_peer(k), device_id_type=MESH,
        )

    w_copy.wait_recv()
    w_half[...] = w_part[core] + w_sib[...]

    def plane_send(k, carry):
        pltpu.make_async_remote_copy(
            src_ref=w_half.at[(u + k) % PLANE], dst_ref=w_plane.at[k],
            send_sem=p1s_sem.at[k], recv_sem=p1r_sem.at[k], device_id=plane_peer(k), device_id_type=MESH,
        ).start()
        return carry

    lax.fori_loop(1, PLANE, plane_send, 0)
    for k in (2, 1, 3):
        sib_copy(k).wait_recv()
        dest = (yl + k) % YL
        outgoing[k] = both(dest * CORES + core, dest).astype(jnp.bfloat16)
        out_copy(k).start()

    def plane_sum(k, total):
        pltpu.make_async_remote_copy(
            src_ref=w_half.at[(u + k) % PLANE], dst_ref=w_plane.at[k],
            send_sem=p1s_sem.at[k], recv_sem=p1r_sem.at[k], device_id=plane_peer(k), device_id_type=MESH,
        ).wait_recv()
        return total + w_plane[k]

    w_unit[y] = lax.fori_loop(1, PLANE, plane_sum, w_half[u])

    def y_copy(k, landed):
        slot = (y + Y - k) % Y if landed else y
        return pltpu.make_async_remote_copy(
            src_ref=w_unit.at[y], dst_ref=w_unit.at[slot],
            send_sem=us_sem.at[k], recv_sem=ur_sem.at[k], device_id=y_peer(k), device_id_type=MESH,
        )

    y_sent = [y_copy(k, False) for k in (4, 3, 5, 2, 6, 1, 7)]
    for copy in y_sent:
        copy.start()
    for k in range(1, Y):
        y_copy(k, True).wait_recv()
    total = w_unit[0]
    for k in range(1, Y):
        total += w_unit[k]
    w_full[core, u] = total

    def spread(k, landed):
        unit = w_full.at[core, (u + PLANE - k) % PLANE if landed else u]
        return pltpu.make_async_remote_copy(
            src_ref=unit, dst_ref=unit,
            send_sem=p2s_sem.at[k], recv_sem=p2r_sem.at[k], device_id=plane_peer(k), device_id_type=MESH,
        )

    def spread_start(k, carry):
        spread(k, False).start()
        return carry

    def spread_wait(k, carry):
        spread(k, True).wait_recv()
        return carry

    lax.fori_loop(1, PLANE, spread_start, 0)
    lax.fori_loop(1, PLANE, spread_wait, 0)

    def last_copy(index):
        return pltpu.make_async_remote_copy(
            src_ref=w_full.at[index], dst_ref=w_full.at[index], send_sem=w4_sem.at[0], recv_sem=w4_sem.at[1],
            device_id=sibling, device_id_type=MESH,
        )

    final = last_copy(core)
    final.start()

    sib_copy(0).wait_recv()
    node_grad = both(rep, yl)
    for k in range(1, YL):
        out_copy(k).wait_recv()
        node_grad += incoming[k].astype(jnp.float32)
    dx_ref[...] = lax.dot_general(
        node_grad.astype(jnp.bfloat16), weight_ref[...], (((1,), (1,)), ((), ())),
        preferred_element_type=jnp.float32,
    ).astype(jnp.bfloat16)

    last_copy(1 - core).wait_recv()
    for half in range(2):
        for h in range(2):
            dw_ref[half * TILE:(half + 1) * TILE, h * TILE:(h + 1) * TILE] = (
                w_full[half, h * 16:(h + 1) * 16].reshape(TILE, TILE)
            )

    for copy in sent + [across_copy] + node_sent + sib_sent + [w_copy, final] + y_sent:
        copy.wait_send()
    for k in range(1, YL):
        out_copy(k).wait_send()

    def drain(k, carry):
        pltpu.make_async_remote_copy(
            src_ref=w_half.at[(u + k) % PLANE], dst_ref=w_plane.at[k],
            send_sem=p1s_sem.at[k], recv_sem=p1r_sem.at[k], device_id=plane_peer(k), device_id_type=MESH,
        ).wait_send()
        spread(k, False).wait_send()
        return carry

    lax.fori_loop(1, PLANE, drain, 0)


def shards(out_grad, node_input, weight, tile_vals, tile_rows, tile_cols, tile_count):
    vmem = pl.BlockSpec(memory_space=pltpu.VMEM)
    hbm = pl.BlockSpec(memory_space=pl.ANY)
    f32, bf16 = jnp.float32, jnp.bfloat16
    dma = pltpu.SemaphoreType.DMA
    slab = YL * CORES * ROWS
    meta = pl.pallas_call(
        schedule,
        out_shape=jax.ShapeDtypeStruct((8, TILE), jnp.int32),
        in_specs=[vmem] * 3,
        out_specs=vmem,
    )(tile_rows.reshape(1, CAP), tile_cols.reshape(1, CAP), tile_count.reshape(1, 1))
    return pl.pallas_call(
        kernel,
        out_shape=(
            jax.ShapeDtypeStruct((ROWS, F), bf16),
            jax.ShapeDtypeStruct((F, F), f32),
        ),
        in_specs=[hbm, hbm, vmem, hbm, pl.BlockSpec(memory_space=pltpu.SMEM)],
        out_specs=(vmem, vmem),
        scratch_shapes=[
            pltpu.VMEM((PLANE * YH * UNITS, UNIT, F), bf16),
            pltpu.VMEM((CAP, TILE, TILE), bf16),
            pltpu.VMEM((CAP + 1, TILE, F), f32),
            pltpu.VMEM((slab, F), bf16),
            pltpu.VMEM((slab, F), bf16),
            pltpu.VMEM((YL * CORES, ROWS, F), bf16),
            pltpu.VMEM((F, slab), bf16),
            pltpu.VMEM((YL, ROWS, F), bf16),
            pltpu.VMEM((YL, ROWS, F), bf16),
            pltpu.VMEM((YL, ROWS, F), bf16),
            pltpu.VMEM((2, PLANE, 8, TILE), f32),
            pltpu.VMEM((PLANE, 8, TILE), f32),
            pltpu.VMEM((PLANE, 8, TILE), f32),
            pltpu.VMEM((PLANE, 8, TILE), f32),
            pltpu.VMEM((Y, 8, TILE), f32),
            pltpu.VMEM((Y, 8, TILE), f32),
            pltpu.VMEM((2, PLANE, 8, TILE), f32),
            dma((3,)),
            dma((len(EDGES),)), dma((len(EDGES),)),
            dma((1,)), dma((1,)),
            dma((2 * YL,)), dma((2 * YL,)),
            dma((YL,)), dma((YL,)),
            dma((YL,)), dma((YL,)),
            dma((2,)),
            dma((PLANE,)), dma((PLANE,)),
            dma((Y,)), dma((Y,)),
            dma((PLANE,)), dma((PLANE,)),
            dma((2,)),
        ],
        compiler_params=pltpu.CompilerParams(
            collective_id=0, has_side_effects=True, vmem_limit_bytes=48 * 1024 * 1024
        ),
        cost_estimate=pl.CostEstimate(flops=2_000_000_000, bytes_accessed=5_000_000, transcendentals=0),
    )(
        out_grad.reshape(UNITS, UNIT, F),
        node_input,
        weight,
        tile_vals.reshape(CAP, TILE, TILE),
        meta,
    )


def solution(mesh):
    placed = (
        P(("rep", "row"), None),
        P(("row", "rep"), None),
        P(),
        P("row", "rep", None, None, None),
        P("row", "rep", None),
        P("row", "rep", None),
        P("row", "rep"),
    )
    return jax.shard_map(
        shards,
        mesh=mesh,
        in_specs=placed,
        out_specs=(P(("row", "rep"), None), P()),
        check_vma=False,
    )
```

```python
import heapq

import jax
import jax.numpy as jnp
from jax import lax
from jax.experimental import pallas as pl
from jax.experimental.pallas import tpu as pltpu
from jax.sharding import PartitionSpec as P

MESH = pl.DeviceIdType.MESH
Z, X, YH, YL, CORES = 8, 4, 2, 4, 2
PLANE = Z * X
Y = YH * YL
TILE = 128
CAP = 128
F = 256
ROWS = 256
UNIT = 16
UNITS = ROWS // UNIT
FIRST = (96, 112)
ACROSS_US = 16.0
LINK_FROM, LINK_STEPS = 12, 16


def gather_edges():
    edges = []

    def chain(rnd, part, axis, base, tie):
        half = (Z if axis == 0 else X) // 2

        def at(k):
            return (base[0] + k, base[1]) if axis == 0 else (base[0], base[1] + k)

        for k in range(1, half + (tie > 0)):
            edges.append((rnd, part, at(k - 1), at(k), axis, 1))
        for k in range(1, half + (tie < 0)):
            edges.append((rnd, part, at(1 - k), at(-k), axis, -1))

    for rnd in (0, 1):
        tie = 1 if rnd == 0 else -1
        chain(rnd, 0, 1, (0, 0), tie)
        for dx in (-1, 0, 1, 2 * tie):
            chain(rnd, 0, 0, (0, dx), 1 if dx in (0, 1) else -1)
        chain(rnd, 1, 0, (0, 0), tie)
        for dz in (-3, -2, -1, 0, 1, 2, 3, 4 * tie):
            chain(rnd, 1, 1, (dz, 0), 1 if 0 <= dz <= 3 else -1)
    return edges


def part_rows(rnd, part):
    return (0, FIRST[rnd]) if part == 0 else (FIRST[rnd], ROWS - FIRST[rnd])


def gather_order(edges):
    kids = {}
    for i, (rnd, part, frm, to, axis, way) in enumerate(edges):
        kids.setdefault((rnd, part, frm), []).append(i)

    def size(i):
        rnd, part, _, to, _, _ = edges[i]
        return 1 + sum(size(j) for j in kids.get((rnd, part, to), []))

    queue = [(0.0, 0, (0, 0, (0, 0)), -1), (0.0, 1, (0, 1, (0, 0)), -1)]
    queue += [(ACROSS_US, 2, (1, 0, (0, 0)), -1), (ACROSS_US, 3, (1, 1, (0, 0)), -1)]
    free, count, order = {}, 4, []
    while queue:
        now, _, node, via = heapq.heappop(queue)
        starts = sorted(kids.get(node, []), key=lambda i: -size(i))
        order.append((node, via, starts))
        for i in starts:
            rnd, part, _, to, axis, way = edges[i]
            begin = max(now, free.get((axis, way), 0.0))
            end = begin + part_rows(rnd, part)[1] * 0.01024
            free[(axis, way)] = end
            heapq.heappush(queue, (end + 1.0, count, (rnd, part, to), i))
            count += 1
    return order


EDGES = gather_edges()
ORDER = gather_order(EDGES)


def kernel(
    grad_ref, node_ref, weight_ref, vals_ref, rows_ref, cols_ref, count_ref,
    dx_ref, dw_ref,
    grads, tiles, sums, high, low, nodes, nodes_t, sib, outgoing, incoming,
    w_part, w_sib, w_half, w_plane, w_unit, w_y, w_full, weights, earlier, latest,
    local_sem, gs_sem, gr_sem, ys_sem, yr_sem, ns_sem, nr_sem, ss_sem, sr_sem,
    rs_sem, rr_sem, w0_sem, p1s_sem, p1r_sem, us_sem, ur_sem, p2s_sem, p2r_sem, w4_sem,
):
    me = lax.axis_index("row")
    rep = lax.axis_index("rep")
    z, x, yh = me // (X * YH), (me // YH) % X, me % YH
    yl, core = rep // CORES, rep % CORES
    y = yh * YL + yl
    u = z * X + x
    sibling = (me, rep + 1 - 2 * core)

    def plane_peer(k):
        return ((u + k) % PLANE * YH + yh, rep)

    def y_peer(k):
        other = (y + k) % Y
        return (u * YH + other // YL, other % YL * CORES + core)

    def rep_peer(k):
        return (me, (yl + k) % YL * CORES + core)

    own_copies = [
        pltpu.make_async_copy(grad_ref, grads.at[pl.ds(me * UNITS, UNITS)], local_sem.at[0]),
        pltpu.make_async_copy(node_ref, nodes.at[rep], local_sem.at[1]),
        pltpu.make_async_copy(vals_ref, tiles, local_sem.at[2]),
        pltpu.make_async_copy(weight_ref, weights, local_sem.at[3]),
    ]
    for copy in own_copies:
        copy.start()

    barrier = pltpu.get_barrier_semaphore()

    def greet(k, carry):
        pl.semaphore_signal(barrier, inc=1, device_id=plane_peer(k), device_id_type=MESH)
        return carry

    lax.fori_loop(1, PLANE, greet, 0)
    for k in range(1, Y):
        pl.semaphore_signal(barrier, inc=1, device_id=y_peer(k), device_id_type=MESH)
    pl.semaphore_signal(barrier, inc=1, device_id=sibling, device_id_type=MESH)
    pl.semaphore_wait(barrier, PLANE - 1 + Y - 1 + 1)

    def piece(rnd, part, offset):
        pz, px = (z - offset[0] + Z) % Z, (x - offset[1] + X) % X
        py = yh if rnd == 0 else 1 - yh
        begin, size = part_rows(rnd, part)
        return grads.at[pl.ds(((pz * X + px) * YH + py) * UNITS + begin // UNIT, size // UNIT)]

    def hop(i, landed):
        rnd, part, frm, to, axis, way = EDGES[i]
        ref = piece(rnd, part, to if landed else frm)
        nz = (z + way + Z) % Z if axis == 0 else z
        nx = (x + way + X) % X if axis == 1 else x
        return pltpu.make_async_remote_copy(
            src_ref=ref, dst_ref=ref, send_sem=gs_sem.at[i], recv_sem=gr_sem.at[i],
            device_id=((nz * X + nx) * YH + yh, rep), device_id_type=MESH,
        )

    def link(t, carry):
        row = rows_ref[0, t]
        earlier[t] = latest[row]
        live = (t < count_ref[0, 0]).astype(jnp.int32)
        for s in range(16):
            now = latest[s]
            latest[s] = now + (row == s).astype(jnp.int32) * live * (t + 1 - now)
        return carry

    own_copies[0].wait()
    partner = ((u * YH) + 1 - yh, rep)

    def across(index):
        ref = grads.at[pl.ds((u * YH + index) * UNITS, UNITS)]
        return pltpu.make_async_remote_copy(
            src_ref=ref, dst_ref=ref, send_sem=ys_sem.at[0], recv_sem=yr_sem.at[0],
            device_id=partner, device_id_type=MESH,
        )

    def node_copy(k, landed):
        block = nodes.at[rep_peer(YL - k)[1] if landed else rep]
        return pltpu.make_async_remote_copy(
            src_ref=block, dst_ref=block, send_sem=ns_sem.at[k], recv_sem=nr_sem.at[k],
            device_id=rep_peer(k), device_id_type=MESH,
        )

    def node_pass(k, landed):
        source = rep_peer(YL - k)[1]
        block = nodes.at[source + 1 - 2 * core if landed else source]
        return pltpu.make_async_remote_copy(
            src_ref=block, dst_ref=block, send_sem=ns_sem.at[YL + k], recv_sem=nr_sem.at[YL + k],
            device_id=sibling, device_id_type=MESH,
        )

    node_sent = [node_copy(k, False) for k in range(1, YL)] + [node_pass(0, False)]
    sent = []
    for step, (node, via, starts) in enumerate([entry for entry in ORDER if entry[2]]):
        if via >= 0:
            hop(via, True).wait_recv()
        elif node == (1, 0, (0, 0)):
            across(1 - yh).wait_recv()
        for i in starts:
            copy = hop(i, False)
            copy.start()
            sent.append(copy)
        if step == 1:
            across_copy = across(yh)
            across_copy.start()
            own_copies[1].wait()
            for row in range(16):
                latest[row] = 0
            sums[0] = jnp.zeros((TILE, F), jnp.float32)
        elif node == (1, 1, (0, 0)):
            for copy in node_sent:
                copy.start()
        if LINK_FROM <= step < LINK_FROM + LINK_STEPS:
            begin = (step - LINK_FROM) * (CAP // LINK_STEPS)
            lax.fori_loop(begin, begin + CAP // LINK_STEPS, link, 0)

    for k in range(1, YL):
        node_copy(k, True).wait_recv()
        copy = node_pass(k, False)
        copy.start()
        node_sent.append(copy)
    for k in range(YL):
        node_pass(k, True).wait_recv()
    for q in range(YL * CORES):
        nodes_t[:, q * ROWS:(q + 1) * ROWS] = nodes[q].T
    own_copies[2].wait()
    for node, via, starts in ORDER:
        if not starts:
            hop(via, True).wait_recv()

    def tile_step(i, carry):
        unit = cols_ref[0, i] * (TILE // UNIT)
        block = jnp.concatenate([grads[unit + j] for j in range(TILE // UNIT)], axis=0)
        product = jnp.dot(tiles[i], block, preferred_element_type=jnp.float32)
        sums[i + 1] = sums[earlier[i]] + product
        return carry

    lax.fori_loop(0, CAP, tile_step, 0, unroll=8)

    def take_sum(s, carry):
        total = sums[latest[s]]
        top = total.astype(jnp.bfloat16)
        at = pl.ds(pl.multiple_of(s * TILE, TILE), TILE)
        high[at] = top
        low[at] = (total - top.astype(jnp.float32)).astype(jnp.bfloat16)
        return carry

    lax.fori_loop(0, 16, take_sum, 0, unroll=2)

    def block_of(index):
        return pl.ds(pl.multiple_of(index * ROWS, ROWS), ROWS)

    def sib_copy(k):
        dest = (yl + k) % YL
        return pltpu.make_async_remote_copy(
            src_ref=high.at[block_of(dest * CORES + 1 - core)], dst_ref=sib.at[dest],
            send_sem=ss_sem.at[k], recv_sem=sr_sem.at[k], device_id=sibling, device_id_type=MESH,
        )

    sib_sent = [sib_copy(k) for k in (2, 1, 3, 0)]
    for copy in sib_sent:
        copy.start()

    def w_dot(half):
        left = nodes_t[pl.ds(pl.multiple_of(half * TILE, TILE), TILE)]
        term = jnp.dot(left, high[...], preferred_element_type=jnp.float32)
        term += jnp.dot(left, low[...], preferred_element_type=jnp.float32)
        for h in range(2):
            w_part[half, h * 16:(h + 1) * 16] = term[:, h * TILE:(h + 1) * TILE].reshape(16, 8, TILE)

    w_dot(1 - core)
    w_copy = pltpu.make_async_remote_copy(
        src_ref=w_part.at[1 - core], dst_ref=w_sib, send_sem=w0_sem.at[0], recv_sem=w0_sem.at[1],
        device_id=sibling, device_id_type=MESH,
    )
    w_copy.start()
    w_dot(core)

    def both(index, at):
        rows = block_of(index)
        return high[rows].astype(jnp.float32) + low[rows].astype(jnp.float32) + sib[at].astype(jnp.float32)

    def out_copy(k):
        return pltpu.make_async_remote_copy(
            src_ref=outgoing.at[k], dst_ref=incoming.at[k], send_sem=rs_sem.at[k], recv_sem=rr_sem.at[k],
            device_id=rep_peer(k), device_id_type=MESH,
        )

    def send_block(k):
        sib_copy(k).wait_recv()
        dest = (yl + k) % YL
        outgoing[k] = both(dest * CORES + core, dest).astype(jnp.bfloat16)
        out_copy(k).start()

    send_block(2)
    w_copy.wait_recv()
    w_half[...] = w_part[core] + w_sib[...]

    def plane_send(k, carry):
        pltpu.make_async_remote_copy(
            src_ref=w_half.at[(u + k) % PLANE], dst_ref=w_plane.at[k],
            send_sem=p1s_sem.at[k], recv_sem=p1r_sem.at[k], device_id=plane_peer(k), device_id_type=MESH,
        ).start()
        return carry

    lax.fori_loop(1, PLANE, plane_send, 0)
    for copy in sent + [across_copy] + node_sent:
        copy.wait_send()

    def plane_sum(k, total):
        pltpu.make_async_remote_copy(
            src_ref=w_half.at[(u + k) % PLANE], dst_ref=w_plane.at[k],
            send_sem=p1s_sem.at[k], recv_sem=p1r_sem.at[k], device_id=plane_peer(k), device_id_type=MESH,
        ).wait_recv()
        return total + w_plane[k]

    w_unit[y] = lax.fori_loop(1, PLANE, plane_sum, w_half[u])

    def y_copy(k, landed):
        slot = (y + Y - k) % Y if landed else y
        return pltpu.make_async_remote_copy(
            src_ref=w_unit.at[y], dst_ref=w_unit.at[slot],
            send_sem=us_sem.at[k], recv_sem=ur_sem.at[k], device_id=y_peer(k), device_id_type=MESH,
        )

    y_sent = [y_copy(k, False) for k in (4, 3, 5, 2, 6, 1, 7)]
    for copy in y_sent:
        copy.start()
    for k in (1, 3):
        send_block(k)
    for k in range(1, Y):
        y_copy(k, True).wait_recv()
    total = w_unit[0]
    for k in range(1, Y):
        total += w_unit[k]
    w_full[core, u] = total

    def spread(k, landed):
        unit = w_full.at[core, (u + PLANE - k) % PLANE if landed else u]
        return pltpu.make_async_remote_copy(
            src_ref=unit, dst_ref=unit,
            send_sem=p2s_sem.at[k], recv_sem=p2r_sem.at[k], device_id=plane_peer(k), device_id_type=MESH,
        )

    def spread_start(k, carry):
        spread(k, False).start()
        return carry

    def spread_wait(k, carry):
        spread(k, True).wait_recv()
        return carry

    lax.fori_loop(1, PLANE, spread_start, 0)
    lax.fori_loop(1, PLANE, spread_wait, 0)

    def last_copy(index):
        return pltpu.make_async_remote_copy(
            src_ref=w_full.at[index], dst_ref=w_full.at[index], send_sem=w4_sem.at[0], recv_sem=w4_sem.at[1],
            device_id=sibling, device_id_type=MESH,
        )

    final = last_copy(core)
    final.start()

    own_copies[3].wait()
    sib_copy(0).wait_recv()
    node_grad = both(rep, yl)
    for k in range(1, YL):
        out_copy(k).wait_recv()
        node_grad += incoming[k].astype(jnp.float32)
    dx_ref[...] = lax.dot_general(
        node_grad.astype(jnp.bfloat16), weights[...], (((1,), (1,)), ((), ())),
        preferred_element_type=jnp.float32,
    ).astype(jnp.bfloat16)

    last_copy(1 - core).wait_recv()
    for half in range(2):
        for h in range(2):
            dw_ref[half * TILE:(half + 1) * TILE, h * TILE:(h + 1) * TILE] = (
                w_full[half, h * 16:(h + 1) * 16].reshape(TILE, TILE)
            )

    for copy in sib_sent + [w_copy, final] + y_sent:
        copy.wait_send()
    for k in range(1, YL):
        out_copy(k).wait_send()

    def drain(k, carry):
        pltpu.make_async_remote_copy(
            src_ref=w_half.at[(u + k) % PLANE], dst_ref=w_plane.at[k],
            send_sem=p1s_sem.at[k], recv_sem=p1r_sem.at[k], device_id=plane_peer(k), device_id_type=MESH,
        ).wait_send()
        spread(k, False).wait_send()
        return carry

    lax.fori_loop(1, PLANE, drain, 0)


def shards(out_grad, node_input, weight, tile_vals, tile_rows, tile_cols, tile_count):
    vmem = pl.BlockSpec(memory_space=pltpu.VMEM)
    hbm = pl.BlockSpec(memory_space=pl.ANY)
    f32, bf16 = jnp.float32, jnp.bfloat16
    dma = pltpu.SemaphoreType.DMA
    slab = YL * CORES * ROWS
    return pl.pallas_call(
        kernel,
        out_shape=(
            jax.ShapeDtypeStruct((ROWS, F), bf16),
            jax.ShapeDtypeStruct((F, F), f32),
        ),
        in_specs=[hbm] * 4 + [pl.BlockSpec(memory_space=pltpu.SMEM)] * 3,
        out_specs=(vmem, vmem),
        scratch_shapes=[
            pltpu.VMEM((PLANE * YH * UNITS, UNIT, F), bf16),
            pltpu.VMEM((CAP, TILE, TILE), bf16),
            pltpu.VMEM((CAP + 1, TILE, F), f32),
            pltpu.VMEM((slab, F), bf16),
            pltpu.VMEM((slab, F), bf16),
            pltpu.VMEM((YL * CORES, ROWS, F), bf16),
            pltpu.VMEM((F, slab), bf16),
            pltpu.VMEM((YL, ROWS, F), bf16),
            pltpu.VMEM((YL, ROWS, F), bf16),
            pltpu.VMEM((YL, ROWS, F), bf16),
            pltpu.VMEM((2, PLANE, 8, TILE), f32),
            pltpu.VMEM((PLANE, 8, TILE), f32),
            pltpu.VMEM((PLANE, 8, TILE), f32),
            pltpu.VMEM((PLANE, 8, TILE), f32),
            pltpu.VMEM((Y, 8, TILE), f32),
            pltpu.VMEM((Y, 8, TILE), f32),
            pltpu.VMEM((2, PLANE, 8, TILE), f32),
            pltpu.VMEM((F, F), bf16),
            pltpu.SMEM((CAP,), jnp.int32),
            pltpu.SMEM((16,), jnp.int32),
            dma((4,)),
            dma((len(EDGES),)), dma((len(EDGES),)),
            dma((1,)), dma((1,)),
            dma((2 * YL,)), dma((2 * YL,)),
            dma((YL,)), dma((YL,)),
            dma((YL,)), dma((YL,)),
            dma((2,)),
            dma((PLANE,)), dma((PLANE,)),
            dma((Y,)), dma((Y,)),
            dma((PLANE,)), dma((PLANE,)),
            dma((2,)),
        ],
        compiler_params=pltpu.CompilerParams(
            collective_id=0, has_side_effects=True, vmem_limit_bytes=62 * 1024 * 1024
        ),
        cost_estimate=pl.CostEstimate(flops=2_000_000_000, bytes_accessed=5_000_000, transcendentals=0),
    )(
        out_grad.reshape(UNITS, UNIT, F),
        node_input,
        weight,
        tile_vals.reshape(CAP, TILE, TILE),
        tile_rows.reshape(1, CAP),
        tile_cols.reshape(1, CAP),
        tile_count.reshape(1, 1),
    )


def solution(mesh):
    placed = (
        P(("rep", "row"), None),
        P(("row", "rep"), None),
        P(),
        P("row", "rep", None, None, None),
        P("row", "rep", None),
        P("row", "rep", None),
        P("row", "rep"),
    )
    return jax.shard_map(
        shards,
        mesh=mesh,
        in_specs=placed,
        out_specs=(P(("row", "rep"), None), P()),
        check_vma=False,
    )
```

```python
import heapq

import jax
import jax.numpy as jnp
from jax import lax
from jax.experimental import pallas as pl
from jax.experimental.pallas import tpu as pltpu
from jax.sharding import PartitionSpec as P

MESH = pl.DeviceIdType.MESH
Z, X, YH, YL, CORES = 8, 4, 2, 4, 2
PLANE = Z * X
Y = YH * YL
TILE = 128
CAP = 128
F = 256
ROWS = 256
UNIT = 16
UNITS = ROWS // UNIT
PARTS = (
    ((True, 96, 1), (False, 80, 1), (False, 80, -1)),
    ((True, 112, -1), (False, 80, 1), (False, 64, -1)),
)
ACROSS_US, HOP_US, LEAD_US = 11.0, 3.0, 1.0
LINK_FROM, LINK_STEPS = 48, 16
CHAINS = 2
SPAN = CAP // CHAINS


def gather_edges():
    edges = []

    def chain(rnd, part, axis, base, tie):
        half = (Z if axis == 0 else X) // 2

        def at(k):
            return (base[0] + k, base[1]) if axis == 0 else (base[0], base[1] + k)

        for k in range(1, half + (tie > 0)):
            edges.append((rnd, part, at(k - 1), at(k), axis, 1))
        for k in range(1, half + (tie < 0)):
            edges.append((rnd, part, at(1 - k), at(-k), axis, -1))

    for rnd, parts in enumerate(PARTS):
        for part, (x_first, _, tie) in enumerate(parts):
            if x_first:
                chain(rnd, part, 1, (0, 0), tie)
                for dx in (-1, 0, 1, 2 * tie):
                    chain(rnd, part, 0, (0, dx), 1 if dx in (0, 1) else -1)
            else:
                chain(rnd, part, 0, (0, 0), tie)
                for dz in (-3, -2, -1, 0, 1, 2, 3, 4 * tie):
                    chain(rnd, part, 1, (dz, 0), 1 if 0 <= dz <= 3 else -1)
    return edges


def part_rows(rnd, part):
    return sum(rows for _, rows, _ in PARTS[rnd][:part]), PARTS[rnd][part][1]


def gather_order(edges):
    kids = {}
    for i, (rnd, part, frm, to, axis, way) in enumerate(edges):
        kids.setdefault((rnd, part, frm), []).append(i)

    def behind(i):
        rnd, part, _, to, _, _ = edges[i]
        below = [behind(j) for j in kids.get((rnd, part, to), [])]
        return 1 + max([b[0] for b in below], default=0), 1 + sum(b[1] for b in below)

    rank = [tuple(-value for value in behind(i)) for i in range(len(edges))]
    events, count, items = [], 0, []

    def at(time, node, via, link):
        nonlocal count
        heapq.heappush(events, (time, count, node, via, link))
        count += 1

    for rnd in range(2):
        for part in range(len(PARTS[rnd])):
            at(ACROSS_US * rnd, (rnd, part, (0, 0)), -1, None)
    links = [(axis, way) for axis in (0, 1) for way in (1, -1)]
    ready, busy = {link: [] for link in links}, {link: False for link in links}
    while events:
        now = events[0][0]
        while events and events[0][0] <= now + 1e-9:
            time, _, node, via, link = heapq.heappop(events)
            if link is not None:
                busy[link] = False
                continue
            if via < 0 or kids.get(node):
                items.append((time, 0, len(items), node, via))
            for i in kids.get(node, []):
                heapq.heappush(ready[edges[i][4:]], (rank[i], i, time))
        for link in links:
            if ready[link] and not busy[link]:
                _, i, since = heapq.heappop(ready[link])
                rnd, part, _, to, _, _ = edges[i]
                end = now + part_rows(rnd, part)[1] * 0.01024
                busy[link] = True
                items.append((max(since, now - LEAD_US), 1, len(items), None, i))
                at(end, None, -1, link)
                at(end + HOP_US, (rnd, part, to), i, None)
    items.sort(key=lambda item: item[:3])
    passed_on = {(rnd, part, frm) for rnd, part, frm, _, _, _ in edges}
    last = [i for i, edge in enumerate(edges) if (edge[0], edge[1], edge[3]) not in passed_on]
    return [item[3:] for item in items], last


EDGES = gather_edges()
ORDER, LAST = gather_order(EDGES)


def kernel(
    grad_ref, node_ref, weight_ref, vals_ref, rows_ref, cols_ref, count_ref,
    dx_ref, dw_ref,
    grads, tiles, sums, high, low, nodes, nodes_t, sib, outgoing, incoming,
    w_part, w_sib, w_half, w_plane, w_unit, w_y, w_full, weights, earlier, latest,
    local_sem, gs_sem, gr_sem, ys_sem, yr_sem, ns_sem, nr_sem, ss_sem, sr_sem,
    rs_sem, rr_sem, w0_sem, p1s_sem, p1r_sem, us_sem, ur_sem, p2s_sem, p2r_sem, w4_sem,
):
    me = lax.axis_index("row")
    rep = lax.axis_index("rep")
    z, x, yh = me // (X * YH), (me // YH) % X, me % YH
    yl, core = rep // CORES, rep % CORES
    y = yh * YL + yl
    u = z * X + x
    sibling = (me, rep + 1 - 2 * core)

    def plane_peer(k):
        return ((u + k) % PLANE * YH + yh, rep)

    def y_peer(k):
        other = (y + k) % Y
        return (u * YH + other // YL, other % YL * CORES + core)

    def rep_peer(k):
        return (me, (yl + k) % YL * CORES + core)

    own_copies = [
        pltpu.make_async_copy(grad_ref, grads.at[pl.ds(me * UNITS, UNITS)], local_sem.at[0]),
        pltpu.make_async_copy(node_ref, nodes.at[rep], local_sem.at[1]),
        pltpu.make_async_copy(vals_ref, tiles, local_sem.at[2]),
        pltpu.make_async_copy(weight_ref, weights, local_sem.at[3]),
    ]
    for copy in own_copies:
        copy.start()

    barrier = pltpu.get_barrier_semaphore()

    def greet(k, carry):
        pl.semaphore_signal(barrier, inc=1, device_id=plane_peer(k), device_id_type=MESH)
        return carry

    lax.fori_loop(1, PLANE, greet, 0)
    for k in range(1, Y):
        pl.semaphore_signal(barrier, inc=1, device_id=y_peer(k), device_id_type=MESH)
    pl.semaphore_signal(barrier, inc=1, device_id=sibling, device_id_type=MESH)
    pl.semaphore_wait(barrier, PLANE - 1 + Y - 1 + 1)

    def piece(rnd, part, offset):
        pz, px = (z - offset[0] + Z) % Z, (x - offset[1] + X) % X
        py = yh if rnd == 0 else 1 - yh
        begin, size = part_rows(rnd, part)
        return grads.at[pl.ds(((pz * X + px) * YH + py) * UNITS + begin // UNIT, size // UNIT)]

    def hop(i, landed):
        rnd, part, frm, to, axis, way = EDGES[i]
        ref = piece(rnd, part, to if landed else frm)
        nz = (z + way + Z) % Z if axis == 0 else z
        nx = (x + way + X) % X if axis == 1 else x
        return pltpu.make_async_remote_copy(
            src_ref=ref, dst_ref=ref, send_sem=gs_sem.at[i], recv_sem=gr_sem.at[i],
            device_id=((nz * X + nx) * YH + yh, rep), device_id_type=MESH,
        )

    def link(chain):
        def step(t, carry):
            row = rows_ref[0, t]
            earlier[t] = latest[chain * 16 + row]
            live = (t < count_ref[0, 0]).astype(jnp.int32)
            for s in range(16):
                now = latest[chain * 16 + s]
                latest[chain * 16 + s] = now + (row == s).astype(jnp.int32) * live * (t % SPAN + 1 - now)
            return carry

        return step

    own_copies[0].wait()
    partner = ((u * YH) + 1 - yh, rep)

    def across(index):
        ref = grads.at[pl.ds((u * YH + index) * UNITS, UNITS)]
        return pltpu.make_async_remote_copy(
            src_ref=ref, dst_ref=ref, send_sem=ys_sem.at[0], recv_sem=yr_sem.at[0],
            device_id=partner, device_id_type=MESH,
        )

    def node_copy(k, landed):
        block = nodes.at[rep_peer(YL - k)[1] if landed else rep]
        return pltpu.make_async_remote_copy(
            src_ref=block, dst_ref=block, send_sem=ns_sem.at[k], recv_sem=nr_sem.at[k],
            device_id=rep_peer(k), device_id_type=MESH,
        )

    def node_pass(k, landed):
        source = rep_peer(YL - k)[1]
        block = nodes.at[source + 1 - 2 * core if landed else source]
        return pltpu.make_async_remote_copy(
            src_ref=block, dst_ref=block, send_sem=ns_sem.at[YL + k], recv_sem=nr_sem.at[YL + k],
            device_id=sibling, device_id_type=MESH,
        )

    node_sent = [node_copy(k, False) for k in range(1, YL)] + [node_pass(0, False)]
    sent = []
    across_copy = across(yh)
    across_copy.start()
    for row in range(16 * CHAINS):
        latest[row] = 0
    for chain in range(CHAINS):
        sums[chain, 0] = jnp.zeros((TILE, F), jnp.float32)
    own_copies[1].wait()
    for node, i in ORDER:
        if node is None:
            copy = hop(i, False)
            copy.start()
            sent.append(copy)
            share = len(sent) - LINK_FROM
            if 0 <= share < LINK_STEPS:
                tiles_each = CAP // LINK_STEPS
                begin = share * tiles_each
                lax.fori_loop(begin, begin + tiles_each, link(begin // SPAN), 0)
        elif i >= 0:
            hop(i, True).wait_recv()
        elif node == (1, 0, (0, 0)):
            across(1 - yh).wait_recv()
        elif node == (1, len(PARTS[1]) - 1, (0, 0)):
            for copy in node_sent:
                copy.start()

    for k in range(1, YL):
        node_copy(k, True).wait_recv()
        copy = node_pass(k, False)
        copy.start()
        node_sent.append(copy)
    for k in range(YL):
        node_pass(k, True).wait_recv()
    for q in range(YL * CORES):
        nodes_t[:, q * ROWS:(q + 1) * ROWS] = nodes[q].T
    own_copies[2].wait()
    for i in LAST:
        hop(i, True).wait_recv()

    def tile_step(i, carry):
        for chain in range(CHAINS):
            t = chain * SPAN + i
            unit = cols_ref[0, t] * (TILE // UNIT)
            block = jnp.concatenate([grads[unit + j] for j in range(TILE // UNIT)], axis=0)
            product = jnp.dot(tiles[t], block, preferred_element_type=jnp.float32)
            sums[chain, i + 1] = sums[chain, earlier[t]] + product
        return carry

    lax.fori_loop(0, SPAN, tile_step, 0, unroll=4)

    def take_sum(s, carry):
        total = sums[0, latest[s]]
        for chain in range(1, CHAINS):
            total += sums[chain, latest[chain * 16 + s]]
        top = total.astype(jnp.bfloat16)
        at = pl.ds(pl.multiple_of(s * TILE, TILE), TILE)
        high[at] = top
        low[at] = (total - top.astype(jnp.float32)).astype(jnp.bfloat16)
        return carry

    lax.fori_loop(0, 16, take_sum, 0, unroll=2)

    def block_of(index):
        return pl.ds(pl.multiple_of(index * ROWS, ROWS), ROWS)

    def sib_copy(k):
        dest = (yl + k) % YL
        return pltpu.make_async_remote_copy(
            src_ref=high.at[block_of(dest * CORES + 1 - core)], dst_ref=sib.at[dest],
            send_sem=ss_sem.at[k], recv_sem=sr_sem.at[k], device_id=sibling, device_id_type=MESH,
        )

    sib_sent = [sib_copy(k) for k in (2, 1, 3, 0)]
    for copy in sib_sent:
        copy.start()

    def w_dot(half):
        left = nodes_t[pl.ds(pl.multiple_of(half * TILE, TILE), TILE)]
        term = jnp.dot(left, high[...], preferred_element_type=jnp.float32)
        term += jnp.dot(left, low[...], preferred_element_type=jnp.float32)
        for h in range(2):
            w_part[half, h * 16:(h + 1) * 16] = term[:, h * TILE:(h + 1) * TILE].reshape(16, 8, TILE)

    w_dot(1 - core)
    w_copy = pltpu.make_async_remote_copy(
        src_ref=w_part.at[1 - core], dst_ref=w_sib, send_sem=w0_sem.at[0], recv_sem=w0_sem.at[1],
        device_id=sibling, device_id_type=MESH,
    )
    w_copy.start()
    w_dot(core)

    def both(index, at):
        rows = block_of(index)
        return high[rows].astype(jnp.float32) + low[rows].astype(jnp.float32) + sib[at].astype(jnp.float32)

    def out_copy(k):
        return pltpu.make_async_remote_copy(
            src_ref=outgoing.at[k], dst_ref=incoming.at[k], send_sem=rs_sem.at[k], recv_sem=rr_sem.at[k],
            device_id=rep_peer(k), device_id_type=MESH,
        )

    def send_block(k):
        sib_copy(k).wait_recv()
        dest = (yl + k) % YL
        outgoing[k] = both(dest * CORES + core, dest).astype(jnp.bfloat16)
        out_copy(k).start()

    send_block(2)
    w_copy.wait_recv()
    w_half[...] = w_part[core] + w_sib[...]

    def plane_send(k, carry):
        pltpu.make_async_remote_copy(
            src_ref=w_half.at[(u + k) % PLANE], dst_ref=w_plane.at[k],
            send_sem=p1s_sem.at[k], recv_sem=p1r_sem.at[k], device_id=plane_peer(k), device_id_type=MESH,
        ).start()
        return carry

    lax.fori_loop(1, PLANE, plane_send, 0)
    for copy in sent + [across_copy] + node_sent:
        copy.wait_send()

    def plane_sum(k, total):
        pltpu.make_async_remote_copy(
            src_ref=w_half.at[(u + k) % PLANE], dst_ref=w_plane.at[k],
            send_sem=p1s_sem.at[k], recv_sem=p1r_sem.at[k], device_id=plane_peer(k), device_id_type=MESH,
        ).wait_recv()
        return total + w_plane[k]

    w_unit[y] = lax.fori_loop(1, PLANE, plane_sum, w_half[u])

    def y_copy(k, landed):
        slot = (y + Y - k) % Y if landed else y
        return pltpu.make_async_remote_copy(
            src_ref=w_unit.at[y], dst_ref=w_unit.at[slot],
            send_sem=us_sem.at[k], recv_sem=ur_sem.at[k], device_id=y_peer(k), device_id_type=MESH,
        )

    y_sent = [y_copy(k, False) for k in (4, 3, 5, 2, 6, 1, 7)]
    for copy in y_sent:
        copy.start()
    for k in (1, 3):
        send_block(k)
    for k in range(1, Y):
        y_copy(k, True).wait_recv()
    total = w_unit[0]
    for k in range(1, Y):
        total += w_unit[k]
    w_full[core, u] = total

    def spread(k, landed):
        unit = w_full.at[core, (u + PLANE - k) % PLANE if landed else u]
        return pltpu.make_async_remote_copy(
            src_ref=unit, dst_ref=unit,
            send_sem=p2s_sem.at[k], recv_sem=p2r_sem.at[k], device_id=plane_peer(k), device_id_type=MESH,
        )

    def spread_start(k, carry):
        spread(k, False).start()
        return carry

    def spread_wait(k, carry):
        spread(k, True).wait_recv()
        return carry

    lax.fori_loop(1, PLANE, spread_start, 0)
    lax.fori_loop(1, PLANE, spread_wait, 0)

    def last_copy(index):
        return pltpu.make_async_remote_copy(
            src_ref=w_full.at[index], dst_ref=w_full.at[index], send_sem=w4_sem.at[0], recv_sem=w4_sem.at[1],
            device_id=sibling, device_id_type=MESH,
        )

    final = last_copy(core)
    final.start()

    own_copies[3].wait()
    sib_copy(0).wait_recv()
    node_grad = both(rep, yl)
    for k in range(1, YL):
        out_copy(k).wait_recv()
        node_grad += incoming[k].astype(jnp.float32)
    dx_ref[...] = lax.dot_general(
        node_grad.astype(jnp.bfloat16), weights[...], (((1,), (1,)), ((), ())),
        preferred_element_type=jnp.float32,
    ).astype(jnp.bfloat16)

    last_copy(1 - core).wait_recv()
    for half in range(2):
        for h in range(2):
            dw_ref[half * TILE:(half + 1) * TILE, h * TILE:(h + 1) * TILE] = (
                w_full[half, h * 16:(h + 1) * 16].reshape(TILE, TILE)
            )

    for copy in sib_sent + [w_copy, final] + y_sent:
        copy.wait_send()
    for k in range(1, YL):
        out_copy(k).wait_send()

    def drain(k, carry):
        pltpu.make_async_remote_copy(
            src_ref=w_half.at[(u + k) % PLANE], dst_ref=w_plane.at[k],
            send_sem=p1s_sem.at[k], recv_sem=p1r_sem.at[k], device_id=plane_peer(k), device_id_type=MESH,
        ).wait_send()
        spread(k, False).wait_send()
        return carry

    lax.fori_loop(1, PLANE, drain, 0)


def shards(out_grad, node_input, weight, tile_vals, tile_rows, tile_cols, tile_count):
    vmem = pl.BlockSpec(memory_space=pltpu.VMEM)
    hbm = pl.BlockSpec(memory_space=pl.ANY)
    f32, bf16 = jnp.float32, jnp.bfloat16
    dma = pltpu.SemaphoreType.DMA
    slab = YL * CORES * ROWS
    return pl.pallas_call(
        kernel,
        out_shape=(
            jax.ShapeDtypeStruct((ROWS, F), bf16),
            jax.ShapeDtypeStruct((F, F), f32),
        ),
        in_specs=[hbm] * 4 + [pl.BlockSpec(memory_space=pltpu.SMEM)] * 3,
        out_specs=(vmem, vmem),
        scratch_shapes=[
            pltpu.VMEM((PLANE * YH * UNITS, UNIT, F), bf16),
            pltpu.VMEM((CAP, TILE, TILE), bf16),
            pltpu.VMEM((CHAINS, SPAN + 1, TILE, F), f32),
            pltpu.VMEM((slab, F), bf16),
            pltpu.VMEM((slab, F), bf16),
            pltpu.VMEM((YL * CORES, ROWS, F), bf16),
            pltpu.VMEM((F, slab), bf16),
            pltpu.VMEM((YL, ROWS, F), bf16),
            pltpu.VMEM((YL, ROWS, F), bf16),
            pltpu.VMEM((YL, ROWS, F), bf16),
            pltpu.VMEM((2, PLANE, 8, TILE), f32),
            pltpu.VMEM((PLANE, 8, TILE), f32),
            pltpu.VMEM((PLANE, 8, TILE), f32),
            pltpu.VMEM((PLANE, 8, TILE), f32),
            pltpu.VMEM((Y, 8, TILE), f32),
            pltpu.VMEM((Y, 8, TILE), f32),
            pltpu.VMEM((2, PLANE, 8, TILE), f32),
            pltpu.VMEM((F, F), bf16),
            pltpu.SMEM((CAP,), jnp.int32),
            pltpu.SMEM((16 * CHAINS,), jnp.int32),
            dma((4,)),
            dma((len(EDGES),)), dma((len(EDGES),)),
            dma((1,)), dma((1,)),
            dma((2 * YL,)), dma((2 * YL,)),
            dma((YL,)), dma((YL,)),
            dma((YL,)), dma((YL,)),
            dma((2,)),
            dma((PLANE,)), dma((PLANE,)),
            dma((Y,)), dma((Y,)),
            dma((PLANE,)), dma((PLANE,)),
            dma((2,)),
        ],
        compiler_params=pltpu.CompilerParams(
            collective_id=0, has_side_effects=True, vmem_limit_bytes=60 * 1024 * 1024
        ),
        cost_estimate=pl.CostEstimate(flops=2_000_000_000, bytes_accessed=5_000_000, transcendentals=0),
    )(
        out_grad.reshape(UNITS, UNIT, F),
        node_input,
        weight,
        tile_vals.reshape(CAP, TILE, TILE),
        tile_rows.reshape(1, CAP),
        tile_cols.reshape(1, CAP),
        tile_count.reshape(1, 1),
    )


def solution(mesh):
    placed = (
        P(("rep", "row"), None),
        P(("row", "rep"), None),
        P(),
        P("row", "rep", None, None, None),
        P("row", "rep", None),
        P("row", "rep", None),
        P("row", "rep"),
    )
    return jax.shard_map(
        shards,
        mesh=mesh,
        in_specs=placed,
        out_specs=(P(("row", "rep"), None), P()),
        check_vma=False,
    )
```

```python
import functools
import heapq

import jax
import jax.numpy as jnp
from jax import lax
from jax.experimental import pallas as pl
from jax.experimental.pallas import tpu as pltpu
from jax.sharding import PartitionSpec as P

MESH = pl.DeviceIdType.MESH
Z, X, YH, YL, CORES = 8, 4, 2, 4, 2
PLANE = Z * X
Y = YH * YL
TILE = 128
CAP = 128
F = 256
ROWS = 256
UNIT = 16
UNITS = ROWS // UNIT
HALF = F // 2
PARTS = (
    ((True, 96, 1), (False, 160, -1)),
    ((True, 112, -1), (False, 144, 1)),
    ((True, 96, -1), (False, 160, 1)),
    ((True, 112, 1), (False, 144, -1)),
)
START_US, HOP_US, LEAD_US = (0.0, 7.0, 0.0, 13.0), 2.0, 1.0
LINK_FROM, LINK_STEPS = 40, 16
CHAINS = 2
SPAN = CAP // CHAINS
EVERY = 3


def gather_edges():
    edges = []

    def chain(rnd, part, axis, base, tie):
        half = (Z if axis == 0 else X) // 2

        def at(k):
            return (base[0] + k, base[1]) if axis == 0 else (base[0], base[1] + k)

        for k in range(1, half + (tie > 0)):
            edges.append((rnd, part, at(k - 1), at(k), axis, 1))
        for k in range(1, half + (tie < 0)):
            edges.append((rnd, part, at(1 - k), at(-k), axis, -1))

    for rnd, parts in enumerate(PARTS):
        for part, (x_first, _, tie) in enumerate(parts):
            if x_first:
                chain(rnd, part, 1, (0, 0), tie)
                for dx in (-1, 0, 1, 2 * tie):
                    chain(rnd, part, 0, (0, dx), 1 if dx in (0, 1) else -1)
            else:
                chain(rnd, part, 0, (0, 0), tie)
                for dz in (-3, -2, -1, 0, 1, 2, 3, 4 * tie):
                    chain(rnd, part, 1, (dz, 0), 1 if 0 <= dz <= 3 else -1)
    return edges


def part_rows(rnd, part):
    return sum(rows for _, rows, _ in PARTS[rnd][:part]), PARTS[rnd][part][1]


def gather_order(edges):
    kids = {}
    for i, (rnd, part, frm, to, axis, way) in enumerate(edges):
        kids.setdefault((rnd, part, frm), []).append(i)

    def behind(i):
        rnd, part, _, to, _, _ = edges[i]
        below = [behind(j) for j in kids.get((rnd, part, to), [])]
        return 1 + max([b[0] for b in below], default=0), 1 + sum(b[1] for b in below)

    rank = [(edges[i][0] // 2, *(-value for value in behind(i))) for i in range(len(edges))]
    events, count, items, first_half = [], 0, [], 0.0

    def at(time, node, via, link):
        nonlocal count
        heapq.heappush(events, (time, count, node, via, link))
        count += 1

    for rnd in range(len(PARTS)):
        for part in range(len(PARTS[rnd])):
            at(START_US[rnd], (rnd, part, (0, 0)), -1, None)
    links = [(axis, way) for axis in (0, 1) for way in (1, -1)]
    ready, busy = {link: [] for link in links}, {link: False for link in links}
    while events:
        now = events[0][0]
        while events and events[0][0] <= now + 1e-9:
            time, _, node, via, link = heapq.heappop(events)
            if link is not None:
                busy[link] = False
                continue
            if via < 0 or kids.get(node):
                items.append((time, 0, len(items), node, via))
            for i in kids.get(node, []):
                heapq.heappush(ready[edges[i][4:]], (rank[i], i, time))
        for link in links:
            if ready[link] and not busy[link]:
                _, i, since = heapq.heappop(ready[link])
                rnd, part, _, to, _, _ = edges[i]
                end = now + part_rows(rnd, part)[1] * 0.00512
                busy[link] = True
                items.append((max(since, now - LEAD_US), 1, len(items), None, i))
                at(end, None, -1, link)
                at(end + HOP_US, (rnd, part, to), i, None)
                if rnd < 2:
                    first_half = max(first_half, end + HOP_US + 1.0)
    items.append((first_half, 2, len(items), None, -1))
    items.sort(key=lambda item: item[:3])
    passed_on = {(rnd, part, frm) for rnd, part, frm, _, _, _ in edges}
    last = [i for i, edge in enumerate(edges) if (edge[0], edge[1], edge[3]) not in passed_on]
    return [item[3:] for item in items], last


EDGES = gather_edges()
ORDER, LAST = gather_order(EDGES)


def kernel(
    grad_ref, node_ref, vals_ref, rows_ref, cols_ref, count_ref,
    result_ref, w_ref,
    grads_0, grads_1, tiles, sums, high, low, nodes, nodes_t, sib, outgoing, incoming,
    w_part, w_sib, w_half, w_plane, w_unit, w_full, earlier, latest,
    local_sem, gs_sem, gr_sem, ys_sem, yr_sem, ns_sem, nr_sem, ss_sem, sr_sem,
    rs_sem, rr_sem, w0_sem, p1s_sem, p1r_sem, us_sem, ur_sem, p2s_sem, p2r_sem, w4_sem,
):
    me = lax.axis_index("row")
    rep = lax.axis_index("rep")
    z, x, yh = me // (X * YH), (me // YH) % X, me % YH
    yl, core = rep // CORES, rep % CORES
    y = yh * YL + yl
    u = z * X + x
    sibling = (me, rep + 1 - 2 * core)

    def plane_peer(k):
        return ((u + k) % PLANE * YH + yh, rep)

    def y_peer(k):
        other = (y + k) % Y
        return (u * YH + other // YL, other % YL * CORES + core)

    def rep_peer(k):
        return (me, (yl + k) % YL * CORES + core)

    grads = (grads_0, grads_1)
    own_copies = [
        pltpu.make_async_copy(
            grad_ref.at[:, :, pl.ds(0, HALF)], grads[0].at[pl.ds(me * UNITS, UNITS)], local_sem.at[0]
        ),
        pltpu.make_async_copy(node_ref, nodes.at[rep], local_sem.at[1]),
        pltpu.make_async_copy(vals_ref, tiles, local_sem.at[2]),
        pltpu.make_async_copy(
            grad_ref.at[:, :, pl.ds(HALF, HALF)], grads[1].at[pl.ds(me * UNITS, UNITS)], local_sem.at[3]
        ),
    ]
    for copy in own_copies:
        copy.start()

    barrier = pltpu.get_barrier_semaphore()

    def greet(k, carry):
        pl.semaphore_signal(barrier, inc=1, device_id=plane_peer(k), device_id_type=MESH)
        return carry

    lax.fori_loop(1, PLANE, greet, 0)
    for k in range(1, Y):
        pl.semaphore_signal(barrier, inc=1, device_id=y_peer(k), device_id_type=MESH)
    pl.semaphore_signal(barrier, inc=1, device_id=sibling, device_id_type=MESH)
    pl.semaphore_wait(barrier, PLANE - 1 + Y - 1 + 1)

    def piece(rnd, part, offset):
        pz, px = (z - offset[0] + Z) % Z, (x - offset[1] + X) % X
        py = yh if rnd % 2 == 0 else 1 - yh
        begin, size = part_rows(rnd, part)
        return grads[rnd // 2].at[pl.ds(((pz * X + px) * YH + py) * UNITS + begin // UNIT, size // UNIT)]

    def hop(i, landed):
        rnd, part, frm, to, axis, way = EDGES[i]
        ref = piece(rnd, part, to if landed else frm)
        nz = (z + way + Z) % Z if axis == 0 else z
        nx = (x + way + X) % X if axis == 1 else x
        return pltpu.make_async_remote_copy(
            src_ref=ref, dst_ref=ref, send_sem=gs_sem.at[i], recv_sem=gr_sem.at[i],
            device_id=((nz * X + nx) * YH + yh, rep), device_id_type=MESH,
        )

    def link(chain):
        def step(t, carry):
            row = rows_ref[0, t]
            earlier[t] = latest[chain * 16 + row]
            live = (t < count_ref[0, 0]).astype(jnp.int32)
            for s in range(16):
                now = latest[chain * 16 + s]
                latest[chain * 16 + s] = now + (row == s).astype(jnp.int32) * live * (t % SPAN + 1 - now)
            return carry

        return step

    own_copies[0].wait()
    own_copies[3].wait()
    partner = ((u * YH) + 1 - yh, rep)

    def across(h, index):
        ref = grads[h].at[pl.ds((u * YH + index) * UNITS, UNITS)]
        return pltpu.make_async_remote_copy(
            src_ref=ref, dst_ref=ref, send_sem=ys_sem.at[h], recv_sem=yr_sem.at[h],
            device_id=partner, device_id_type=MESH,
        )

    def node_copy(k, landed):
        block = nodes.at[rep_peer(YL - k)[1] if landed else rep]
        return pltpu.make_async_remote_copy(
            src_ref=block, dst_ref=block, send_sem=ns_sem.at[k], recv_sem=nr_sem.at[k],
            device_id=rep_peer(k), device_id_type=MESH,
        )

    def node_pass(k, landed):
        source = rep_peer(YL - k)[1]
        block = nodes.at[source + 1 - 2 * core if landed else source]
        return pltpu.make_async_remote_copy(
            src_ref=block, dst_ref=block, send_sem=ns_sem.at[YL + k], recv_sem=nr_sem.at[YL + k],
            device_id=sibling, device_id_type=MESH,
        )

    node_sent = [node_copy(k, False) for k in range(1, YL)] + [node_pass(0, False)]
    sent = []
    across_sent = [across(h, yh) for h in range(2)]
    for copy in across_sent:
        copy.start()
    for row in range(16 * CHAINS):
        latest[row] = 0
    for chain in range(CHAINS):
        sums[chain, 0] = jnp.zeros((TILE, HALF), jnp.float32)
    own_copies[1].wait()
    def tile_steps(h, begin, count, unroll):
        def step(i, carry):
            for chain in range(CHAINS):
                t = chain * SPAN + i
                unit = cols_ref[0, t] * (TILE // UNIT)
                block = jnp.concatenate([grads[h][unit + j] for j in range(TILE // UNIT)], axis=0)
                product = jnp.dot(tiles[t], block, preferred_element_type=jnp.float32)
                sums[chain, i + 1] = sums[chain, earlier[t]] + product
            return carry

        lax.fori_loop(begin, begin + count, step, 0, unroll=unroll)

    def take_sums(h, begin, count):
        def step(s, carry):
            total = sums[0, latest[s]]
            for chain in range(1, CHAINS):
                total += sums[chain, latest[chain * 16 + s]]
            top = total.astype(jnp.bfloat16)
            at = pl.ds(pl.multiple_of(s * TILE, TILE), TILE)
            high[h, at] = top
            low[h, at] = (total - top.astype(jnp.float32)).astype(jnp.bfloat16)
            return carry

        lax.fori_loop(begin, begin + count, step, 0, unroll=2)

    def block_of(index):
        return pl.ds(pl.multiple_of(index * ROWS, ROWS), ROWS)

    def sib_copy(h, k):
        dest = (yl + k) % YL
        return pltpu.make_async_remote_copy(
            src_ref=high.at[h, block_of(dest * CORES + 1 - core)], dst_ref=sib.at[h, dest],
            send_sem=ss_sem.at[h * YL + k], recv_sem=sr_sem.at[h * YL + k],
            device_id=sibling, device_id_type=MESH,
        )

    def both(h, index, at):
        rows = block_of(index)
        return (
            high[h, rows].astype(jnp.float32) + low[h, rows].astype(jnp.float32) + sib[h, at].astype(jnp.float32)
        )

    def out_copy(h, k):
        return pltpu.make_async_remote_copy(
            src_ref=outgoing.at[h, k], dst_ref=incoming.at[h, k],
            send_sem=rs_sem.at[h * YL + k], recv_sem=rr_sem.at[h * YL + k],
            device_id=rep_peer(k), device_id_type=MESH,
        )

    def sib_start(h):
        for k in (2, 1, 3, 0):
            sib_copy(h, k).start()

    def send_block(h, k):
        sib_copy(h, k).wait_recv()
        dest = (yl + k) % YL
        outgoing[h, k] = both(h, dest * CORES + core, dest).astype(jnp.bfloat16)
        out_copy(h, k).start()

    def w_dot(h, half):
        left = nodes_t[pl.ds(pl.multiple_of(half * TILE, TILE), TILE)]
        term = jnp.dot(left, high[h], preferred_element_type=jnp.float32)
        term += jnp.dot(left, low[h], preferred_element_type=jnp.float32)
        w_part[half, h * 16:(h + 1) * 16] = term.reshape(16, 8, TILE)

    def node_forward():
        for k in range(1, YL):
            node_copy(k, True).wait_recv()
            copy = node_pass(k, False)
            copy.start()
            node_sent.append(copy)
        own_copies[2].wait()

    def node_landed():
        for k in range(YL):
            node_pass(k, True).wait_recv()

    def node_turn(q):
        nodes_t[:, q * ROWS:(q + 1) * ROWS] = nodes[q].T

    shares = [node_forward]
    shares += [functools.partial(tile_steps, 0, begin, 4, True) for begin in range(0, SPAN, 4)]
    shares += [functools.partial(take_sums, 0, begin, 4) for begin in range(0, 16, 4)]
    shares += [functools.partial(sib_start, 0), node_landed]
    shares += [functools.partial(node_turn, q) for q in range(YL * CORES)]
    shares += [functools.partial(send_block, 0, k) for k in (2, 1, 3)]
    shares += [functools.partial(w_dot, 0, half) for half in range(2)]

    since = -1
    for node, i in ORDER:
        if node is None and i < 0:
            for last in LAST:
                if EDGES[last][0] < 2:
                    hop(last, True).wait_recv()
            since = 0
            continue
        if node is None:
            copy = hop(i, False)
            copy.start()
            sent.append(copy)
            share = len(sent) - LINK_FROM
            if 0 <= share < LINK_STEPS:
                tiles_each = CAP // LINK_STEPS
                begin = share * tiles_each
                lax.fori_loop(begin, begin + tiles_each, link(begin // SPAN), 0)
        elif i >= 0:
            hop(i, True).wait_recv()
        elif node[0] % 2 == 1 and node[1] == 0:
            across(node[0] // 2, 1 - yh).wait_recv()
        elif node == (3, len(PARTS[3]) - 1, (0, 0)):
            for copy in node_sent:
                copy.start()
        if since >= 0:
            if since % EVERY == 0 and shares:
                shares.pop(0)()
            since += 1
    while shares:
        shares.pop(0)()
    for last in LAST:
        if EDGES[last][0] >= 2:
            hop(last, True).wait_recv()

    tile_steps(1, 0, SPAN, 4)
    take_sums(1, 0, 16)
    sib_start(1)
    w_dot(1, 1 - core)
    w_copy = pltpu.make_async_remote_copy(
        src_ref=w_part.at[1 - core], dst_ref=w_sib, send_sem=w0_sem.at[0], recv_sem=w0_sem.at[1],
        device_id=sibling, device_id_type=MESH,
    )
    w_copy.start()
    w_dot(1, core)
    send_block(1, 2)
    w_copy.wait_recv()
    w_half[...] = w_part[core] + w_sib[...]

    def plane_send(k, carry):
        pltpu.make_async_remote_copy(
            src_ref=w_half.at[(u + k) % PLANE], dst_ref=w_plane.at[k],
            send_sem=p1s_sem.at[k], recv_sem=p1r_sem.at[k], device_id=plane_peer(k), device_id_type=MESH,
        ).start()
        return carry

    lax.fori_loop(1, PLANE, plane_send, 0)
    for copy in sent + across_sent + node_sent:
        copy.wait_send()

    def plane_sum(k, total):
        pltpu.make_async_remote_copy(
            src_ref=w_half.at[(u + k) % PLANE], dst_ref=w_plane.at[k],
            send_sem=p1s_sem.at[k], recv_sem=p1r_sem.at[k], device_id=plane_peer(k), device_id_type=MESH,
        ).wait_recv()
        return total + w_plane[k]

    w_unit[y] = lax.fori_loop(1, PLANE, plane_sum, w_half[u])

    def y_copy(k, landed):
        slot = (y + Y - k) % Y if landed else y
        return pltpu.make_async_remote_copy(
            src_ref=w_unit.at[y], dst_ref=w_unit.at[slot],
            send_sem=us_sem.at[k], recv_sem=ur_sem.at[k], device_id=y_peer(k), device_id_type=MESH,
        )

    y_sent = [y_copy(k, False) for k in (4, 3, 5, 2, 6, 1, 7)]
    for copy in y_sent:
        copy.start()
    for k in (1, 3):
        send_block(1, k)
    for k in range(1, Y):
        y_copy(k, True).wait_recv()
    total = w_unit[0]
    for k in range(1, Y):
        total += w_unit[k]
    w_full[core, u] = total

    def spread(k, landed):
        unit = w_full.at[core, (u + PLANE - k) % PLANE if landed else u]
        return pltpu.make_async_remote_copy(
            src_ref=unit, dst_ref=unit,
            send_sem=p2s_sem.at[k], recv_sem=p2r_sem.at[k], device_id=plane_peer(k), device_id_type=MESH,
        )

    def spread_start(k, carry):
        spread(k, False).start()
        return carry

    def spread_wait(k, carry):
        spread(k, True).wait_recv()
        return carry

    lax.fori_loop(1, PLANE, spread_start, 0)
    lax.fori_loop(1, PLANE, spread_wait, 0)

    def last_copy(index):
        return pltpu.make_async_remote_copy(
            src_ref=w_full.at[index], dst_ref=w_full.at[index], send_sem=w4_sem.at[0], recv_sem=w4_sem.at[1],
            device_id=sibling, device_id_type=MESH,
        )

    final = last_copy(core)
    final.start()

    for h in range(2):
        sib_copy(h, 0).wait_recv()
        node_grad = both(h, rep, yl)
        for k in range(1, YL):
            out_copy(h, k).wait_recv()
            node_grad += incoming[h, k].astype(jnp.float32)
        result_ref[:, h * HALF:(h + 1) * HALF] = node_grad.astype(jnp.bfloat16)
    last_copy(1 - core).wait_recv()
    w_ref[...] = w_full[...]

    for copy in [w_copy, final] + y_sent:
        copy.wait_send()
    for h in range(2):
        for k in range(YL):
            sib_copy(h, k).wait_send()
        for k in range(1, YL):
            out_copy(h, k).wait_send()

    def drain(k, carry):
        pltpu.make_async_remote_copy(
            src_ref=w_half.at[(u + k) % PLANE], dst_ref=w_plane.at[k],
            send_sem=p1s_sem.at[k], recv_sem=p1r_sem.at[k], device_id=plane_peer(k), device_id_type=MESH,
        ).wait_send()
        spread(k, False).wait_send()
        return carry

    lax.fori_loop(1, PLANE, drain, 0)


def finish(grad_ref, w_ref, weight_ref, dx_ref, dw_ref):
    dx_ref[...] = lax.dot_general(
        grad_ref[...], weight_ref[...], (((1,), (1,)), ((), ())), preferred_element_type=jnp.float32
    ).astype(jnp.bfloat16)
    for half in range(2):
        for h in range(2):
            dw_ref[half * TILE:(half + 1) * TILE, h * TILE:(h + 1) * TILE] = (
                w_ref[half, h * 16:(h + 1) * 16].reshape(TILE, TILE)
            )


def shards(out_grad, node_input, weight, tile_vals, tile_rows, tile_cols, tile_count):
    vmem = pl.BlockSpec(memory_space=pltpu.VMEM)
    hbm = pl.BlockSpec(memory_space=pl.ANY)
    f32, bf16 = jnp.float32, jnp.bfloat16
    dma = pltpu.SemaphoreType.DMA
    slab = YL * CORES * ROWS
    node_grad, w_sum = pl.pallas_call(
        kernel,
        out_shape=(
            jax.ShapeDtypeStruct((ROWS, F), bf16),
            jax.ShapeDtypeStruct((2, PLANE, 8, TILE), f32),
        ),
        in_specs=[hbm] * 3 + [pl.BlockSpec(memory_space=pltpu.SMEM)] * 3,
        out_specs=(vmem, vmem),
        scratch_shapes=[
            pltpu.VMEM((PLANE * YH * UNITS, UNIT, HALF), bf16),
            pltpu.VMEM((PLANE * YH * UNITS, UNIT, HALF), bf16),
            pltpu.VMEM((CAP, TILE, TILE), bf16),
            pltpu.VMEM((CHAINS, SPAN + 1, TILE, HALF), f32),
            pltpu.VMEM((2, slab, HALF), bf16),
            pltpu.VMEM((2, slab, HALF), bf16),
            pltpu.VMEM((YL * CORES, ROWS, F), bf16),
            pltpu.VMEM((F, slab), bf16),
            pltpu.VMEM((2, YL, ROWS, HALF), bf16),
            pltpu.VMEM((2, YL, ROWS, HALF), bf16),
            pltpu.VMEM((2, YL, ROWS, HALF), bf16),
            pltpu.VMEM((2, PLANE, 8, TILE), f32),
            pltpu.VMEM((PLANE, 8, TILE), f32),
            pltpu.VMEM((PLANE, 8, TILE), f32),
            pltpu.VMEM((PLANE, 8, TILE), f32),
            pltpu.VMEM((Y, 8, TILE), f32),
            pltpu.VMEM((2, PLANE, 8, TILE), f32),
            pltpu.SMEM((CAP,), jnp.int32),
            pltpu.SMEM((16 * CHAINS,), jnp.int32),
            dma((4,)),
            dma((len(EDGES),)), dma((len(EDGES),)),
            dma((2,)), dma((2,)),
            dma((2 * YL,)), dma((2 * YL,)),
            dma((2 * YL,)), dma((2 * YL,)),
            dma((2 * YL,)), dma((2 * YL,)),
            dma((2,)),
            dma((PLANE,)), dma((PLANE,)),
            dma((Y,)), dma((Y,)),
            dma((PLANE,)), dma((PLANE,)),
            dma((2,)),
        ],
        compiler_params=pltpu.CompilerParams(
            collective_id=0, has_side_effects=True, vmem_limit_bytes=60 * 1024 * 1024
        ),
        cost_estimate=pl.CostEstimate(flops=2_000_000_000, bytes_accessed=5_000_000, transcendentals=0),
    )(
        out_grad.reshape(UNITS, UNIT, F),
        node_input,
        tile_vals.reshape(CAP, TILE, TILE),
        tile_rows.reshape(1, CAP),
        tile_cols.reshape(1, CAP),
        tile_count.reshape(1, 1),
    )
    return pl.pallas_call(
        finish,
        out_shape=(
            jax.ShapeDtypeStruct((ROWS, F), bf16),
            jax.ShapeDtypeStruct((F, F), f32),
        ),
        in_specs=[vmem] * 3,
        out_specs=(vmem, vmem),
        compiler_params=pltpu.CompilerParams(vmem_limit_bytes=60 * 1024 * 1024),
    )(node_grad, w_sum, weight)


def solution(mesh):
    placed = (
        P(("rep", "row"), None),
        P(("row", "rep"), None),
        P(),
        P("row", "rep", None, None, None),
        P("row", "rep", None),
        P("row", "rep", None),
        P("row", "rep"),
    )
    return jax.shard_map(
        shards,
        mesh=mesh,
        in_specs=placed,
        out_specs=(P(("row", "rep"), None), P()),
        check_vma=False,
    )
```

```python
import heapq

import jax
import jax.numpy as jnp
from jax import lax
from jax.experimental import pallas as pl
from jax.experimental.pallas import tpu as pltpu
from jax.sharding import PartitionSpec as P

MESH = pl.DeviceIdType.MESH
Z, X, YH, YL, CORES = 8, 4, 2, 4, 2
PLANE = Z * X
Y = YH * YL
TILE = 128
CAP = 128
F = 256
ROWS = 256
UNIT = 16
UNITS = ROWS // UNIT
PARTS = (
    ((True, 96, 1), (False, 80, 1), (False, 80, -1)),
    ((True, 112, -1), (False, 80, 1), (False, 64, -1)),
)
ACROSS_US, HOP_US, LEAD_US = 11.0, 3.0, 1.0
LINK_FROM, LINK_STEPS = 48, 16
CHAINS = 2
SPAN = CAP // CHAINS


def gather_edges():
    edges = []

    def chain(rnd, part, axis, base, tie):
        half = (Z if axis == 0 else X) // 2

        def at(k):
            return (base[0] + k, base[1]) if axis == 0 else (base[0], base[1] + k)

        for k in range(1, half + (tie > 0)):
            edges.append((rnd, part, at(k - 1), at(k), axis, 1))
        for k in range(1, half + (tie < 0)):
            edges.append((rnd, part, at(1 - k), at(-k), axis, -1))

    for rnd, parts in enumerate(PARTS):
        for part, (x_first, _, tie) in enumerate(parts):
            if x_first:
                chain(rnd, part, 1, (0, 0), tie)
                for dx in (-1, 0, 1, 2 * tie):
                    chain(rnd, part, 0, (0, dx), 1 if dx in (0, 1) else -1)
            else:
                chain(rnd, part, 0, (0, 0), tie)
                for dz in (-3, -2, -1, 0, 1, 2, 3, 4 * tie):
                    chain(rnd, part, 1, (dz, 0), 1 if 0 <= dz <= 3 else -1)
    return edges


def part_rows(rnd, part):
    return sum(rows for _, rows, _ in PARTS[rnd][:part]), PARTS[rnd][part][1]


def gather_order(edges):
    kids = {}
    for i, (rnd, part, frm, to, axis, way) in enumerate(edges):
        kids.setdefault((rnd, part, frm), []).append(i)

    def behind(i):
        rnd, part, _, to, _, _ = edges[i]
        below = [behind(j) for j in kids.get((rnd, part, to), [])]
        return 1 + max([b[0] for b in below], default=0), 1 + sum(b[1] for b in below)

    rank = [tuple(-value for value in behind(i)) for i in range(len(edges))]
    events, count, items = [], 0, []

    def at(time, node, via, link):
        nonlocal count
        heapq.heappush(events, (time, count, node, via, link))
        count += 1

    for rnd in range(2):
        for part in range(len(PARTS[rnd])):
            at(ACROSS_US * rnd, (rnd, part, (0, 0)), -1, None)
    links = [(axis, way) for axis in (0, 1) for way in (1, -1)]
    ready, busy = {link: [] for link in links}, {link: False for link in links}
    while events:
        now = events[0][0]
        while events and events[0][0] <= now + 1e-9:
            time, _, node, via, link = heapq.heappop(events)
            if link is not None:
                busy[link] = False
                continue
            if via < 0 or kids.get(node):
                items.append((time, 0, len(items), node, via))
            for i in kids.get(node, []):
                heapq.heappush(ready[edges[i][4:]], (rank[i], i, time))
        for link in links:
            if ready[link] and not busy[link]:
                _, i, since = heapq.heappop(ready[link])
                rnd, part, _, to, _, _ = edges[i]
                end = now + part_rows(rnd, part)[1] * 0.01024
                busy[link] = True
                items.append((max(since, now - LEAD_US), 1, len(items), None, i))
                at(end, None, -1, link)
                at(end + HOP_US, (rnd, part, to), i, None)
    items.sort(key=lambda item: item[:3])
    passed_on = {(rnd, part, frm) for rnd, part, frm, _, _, _ in edges}
    last = [i for i, edge in enumerate(edges) if (edge[0], edge[1], edge[3]) not in passed_on]
    return [item[3:] for item in items], last


EDGES = gather_edges()
ORDER, LAST = gather_order(EDGES)


def kernel(
    grad_ref, node_ref, vals_ref, rows_ref, cols_ref, count_ref,
    result_ref, w_ref,
    grads, tiles, sums, high, low, nodes, nodes_t, sib, outgoing, incoming,
    w_part, w_sib, w_half, w_plane, w_unit, w_y, w_full, earlier, latest,
    local_sem, gs_sem, gr_sem, ys_sem, yr_sem, ns_sem, nr_sem, ss_sem, sr_sem,
    rs_sem, rr_sem, w0_sem, p1s_sem, p1r_sem, us_sem, ur_sem, p2s_sem, p2r_sem, w4_sem,
):
    me = lax.axis_index("row")
    rep = lax.axis_index("rep")
    z, x, yh = me // (X * YH), (me // YH) % X, me % YH
    yl, core = rep // CORES, rep % CORES
    y = yh * YL + yl
    u = z * X + x
    sibling = (me, rep + 1 - 2 * core)

    def plane_peer(k):
        return ((u + k) % PLANE * YH + yh, rep)

    def y_peer(k):
        other = (y + k) % Y
        return (u * YH + other // YL, other % YL * CORES + core)

    def rep_peer(k):
        return (me, (yl + k) % YL * CORES + core)

    own_copies = [
        pltpu.make_async_copy(grad_ref, grads.at[pl.ds(me * UNITS, UNITS)], local_sem.at[0]),
        pltpu.make_async_copy(node_ref, nodes.at[rep], local_sem.at[1]),
        pltpu.make_async_copy(vals_ref, tiles, local_sem.at[2]),
    ]
    for copy in own_copies:
        copy.start()

    barrier = pltpu.get_barrier_semaphore()

    def greet(k, carry):
        pl.semaphore_signal(barrier, inc=1, device_id=plane_peer(k), device_id_type=MESH)
        return carry

    lax.fori_loop(1, PLANE, greet, 0)
    for k in range(1, Y):
        pl.semaphore_signal(barrier, inc=1, device_id=y_peer(k), device_id_type=MESH)
    pl.semaphore_signal(barrier, inc=1, device_id=sibling, device_id_type=MESH)
    pl.semaphore_wait(barrier, PLANE - 1 + Y - 1 + 1)

    def piece(rnd, part, offset):
        pz, px = (z - offset[0] + Z) % Z, (x - offset[1] + X) % X
        py = yh if rnd == 0 else 1 - yh
        begin, size = part_rows(rnd, part)
        return grads.at[pl.ds(((pz * X + px) * YH + py) * UNITS + begin // UNIT, size // UNIT)]

    def hop(i, landed):
        rnd, part, frm, to, axis, way = EDGES[i]
        ref = piece(rnd, part, to if landed else frm)
        nz = (z + way + Z) % Z if axis == 0 else z
        nx = (x + way + X) % X if axis == 1 else x
        return pltpu.make_async_remote_copy(
            src_ref=ref, dst_ref=ref, send_sem=gs_sem.at[i], recv_sem=gr_sem.at[i],
            device_id=((nz * X + nx) * YH + yh, rep), device_id_type=MESH,
        )

    def link(chain):
        def step(t, carry):
            row = rows_ref[0, t]
            earlier[t] = latest[chain * 16 + row]
            live = (t < count_ref[0, 0]).astype(jnp.int32)
            for s in range(16):
                now = latest[chain * 16 + s]
                latest[chain * 16 + s] = now + (row == s).astype(jnp.int32) * live * (t % SPAN + 1 - now)
            return carry

        return step

    own_copies[0].wait()
    partner = ((u * YH) + 1 - yh, rep)

    def across(index):
        ref = grads.at[pl.ds((u * YH + index) * UNITS, UNITS)]
        return pltpu.make_async_remote_copy(
            src_ref=ref, dst_ref=ref, send_sem=ys_sem.at[0], recv_sem=yr_sem.at[0],
            device_id=partner, device_id_type=MESH,
        )

    def node_copy(k, landed):
        block = nodes.at[rep_peer(YL - k)[1] if landed else rep]
        return pltpu.make_async_remote_copy(
            src_ref=block, dst_ref=block, send_sem=ns_sem.at[k], recv_sem=nr_sem.at[k],
            device_id=rep_peer(k), device_id_type=MESH,
        )

    def node_pass(k, landed):
        source = rep_peer(YL - k)[1]
        block = nodes.at[source + 1 - 2 * core if landed else source]
        return pltpu.make_async_remote_copy(
            src_ref=block, dst_ref=block, send_sem=ns_sem.at[YL + k], recv_sem=nr_sem.at[YL + k],
            device_id=sibling, device_id_type=MESH,
        )

    node_sent = [node_copy(k, False) for k in range(1, YL)] + [node_pass(0, False)]
    sent = []
    across_copy = across(yh)
    across_copy.start()
    for row in range(16 * CHAINS):
        latest[row] = 0
    for chain in range(CHAINS):
        sums[chain, 0] = jnp.zeros((TILE, F), jnp.float32)
    own_copies[1].wait()
    for node, i in ORDER:
        if node is None:
            copy = hop(i, False)
            copy.start()
            sent.append(copy)
            share = len(sent) - LINK_FROM
            if 0 <= share < LINK_STEPS:
                tiles_each = CAP // LINK_STEPS
                begin = share * tiles_each
                lax.fori_loop(begin, begin + tiles_each, link(begin // SPAN), 0)
        elif i >= 0:
            hop(i, True).wait_recv()
        elif node == (1, 0, (0, 0)):
            across(1 - yh).wait_recv()
        elif node == (1, len(PARTS[1]) - 1, (0, 0)):
            for copy in node_sent:
                copy.start()

    for k in range(1, YL):
        node_copy(k, True).wait_recv()
        copy = node_pass(k, False)
        copy.start()
        node_sent.append(copy)
    for k in range(YL):
        node_pass(k, True).wait_recv()
    for q in range(YL * CORES):
        nodes_t[:, q * ROWS:(q + 1) * ROWS] = nodes[q].T
    own_copies[2].wait()
    for i in LAST:
        hop(i, True).wait_recv()

    def tile_step(i, carry):
        for chain in range(CHAINS):
            t = chain * SPAN + i
            unit = cols_ref[0, t] * (TILE // UNIT)
            block = jnp.concatenate([grads[unit + j] for j in range(TILE // UNIT)], axis=0)
            product = jnp.dot(tiles[t], block, preferred_element_type=jnp.float32)
            sums[chain, i + 1] = sums[chain, earlier[t]] + product
        return carry

    lax.fori_loop(0, SPAN, tile_step, 0, unroll=4)

    def take_sum(s, carry):
        total = sums[0, latest[s]]
        for chain in range(1, CHAINS):
            total += sums[chain, latest[chain * 16 + s]]
        top = total.astype(jnp.bfloat16)
        at = pl.ds(pl.multiple_of(s * TILE, TILE), TILE)
        high[at] = top
        low[at] = (total - top.astype(jnp.float32)).astype(jnp.bfloat16)
        return carry

    lax.fori_loop(0, 16, take_sum, 0, unroll=2)

    def block_of(index):
        return pl.ds(pl.multiple_of(index * ROWS, ROWS), ROWS)

    def sib_copy(k):
        dest = (yl + k) % YL
        return pltpu.make_async_remote_copy(
            src_ref=high.at[block_of(dest * CORES + 1 - core)], dst_ref=sib.at[dest],
            send_sem=ss_sem.at[k], recv_sem=sr_sem.at[k], device_id=sibling, device_id_type=MESH,
        )

    sib_sent = [sib_copy(k) for k in (2, 1, 3, 0)]
    for copy in sib_sent:
        copy.start()

    def w_dot(half):
        left = nodes_t[pl.ds(pl.multiple_of(half * TILE, TILE), TILE)]
        term = jnp.dot(left, high[...], preferred_element_type=jnp.float32)
        term += jnp.dot(left, low[...], preferred_element_type=jnp.float32)
        for h in range(2):
            w_part[half, h * 16:(h + 1) * 16] = term[:, h * TILE:(h + 1) * TILE].reshape(16, 8, TILE)

    w_dot(1 - core)
    w_copy = pltpu.make_async_remote_copy(
        src_ref=w_part.at[1 - core], dst_ref=w_sib, send_sem=w0_sem.at[0], recv_sem=w0_sem.at[1],
        device_id=sibling, device_id_type=MESH,
    )
    w_copy.start()
    w_dot(core)

    def both(index, at):
        rows = block_of(index)
        return high[rows].astype(jnp.float32) + low[rows].astype(jnp.float32) + sib[at].astype(jnp.float32)

    def out_copy(k):
        return pltpu.make_async_remote_copy(
            src_ref=outgoing.at[k], dst_ref=incoming.at[k], send_sem=rs_sem.at[k], recv_sem=rr_sem.at[k],
            device_id=rep_peer(k), device_id_type=MESH,
        )

    def send_block(k):
        sib_copy(k).wait_recv()
        dest = (yl + k) % YL
        outgoing[k] = both(dest * CORES + core, dest).astype(jnp.bfloat16)
        out_copy(k).start()

    send_block(2)
    w_copy.wait_recv()
    w_half[...] = w_part[core] + w_sib[...]

    def plane_send(k, carry):
        pltpu.make_async_remote_copy(
            src_ref=w_half.at[(u + k) % PLANE], dst_ref=w_plane.at[k],
            send_sem=p1s_sem.at[k], recv_sem=p1r_sem.at[k], device_id=plane_peer(k), device_id_type=MESH,
        ).start()
        return carry

    lax.fori_loop(1, PLANE, plane_send, 0)
    for copy in sent + [across_copy] + node_sent:
        copy.wait_send()

    def plane_sum(k, total):
        pltpu.make_async_remote_copy(
            src_ref=w_half.at[(u + k) % PLANE], dst_ref=w_plane.at[k],
            send_sem=p1s_sem.at[k], recv_sem=p1r_sem.at[k], device_id=plane_peer(k), device_id_type=MESH,
        ).wait_recv()
        return total + w_plane[k]

    w_unit[y] = lax.fori_loop(1, PLANE, plane_sum, w_half[u])

    def y_copy(k, landed):
        slot = (y + Y - k) % Y if landed else y
        return pltpu.make_async_remote_copy(
            src_ref=w_unit.at[y], dst_ref=w_unit.at[slot],
            send_sem=us_sem.at[k], recv_sem=ur_sem.at[k], device_id=y_peer(k), device_id_type=MESH,
        )

    y_sent = [y_copy(k, False) for k in (4, 3, 5, 2, 6, 1, 7)]
    for copy in y_sent:
        copy.start()
    for k in (1, 3):
        send_block(k)
    for k in range(1, Y):
        y_copy(k, True).wait_recv()
    total = w_unit[0]
    for k in range(1, Y):
        total += w_unit[k]
    w_full[core, u] = total

    def spread(k, landed):
        unit = w_full.at[core, (u + PLANE - k) % PLANE if landed else u]
        return pltpu.make_async_remote_copy(
            src_ref=unit, dst_ref=unit,
            send_sem=p2s_sem.at[k], recv_sem=p2r_sem.at[k], device_id=plane_peer(k), device_id_type=MESH,
        )

    def spread_start(k, carry):
        spread(k, False).start()
        return carry

    def spread_wait(k, carry):
        spread(k, True).wait_recv()
        return carry

    lax.fori_loop(1, PLANE, spread_start, 0)
    lax.fori_loop(1, PLANE, spread_wait, 0)

    def last_copy(index):
        return pltpu.make_async_remote_copy(
            src_ref=w_full.at[index], dst_ref=w_full.at[index], send_sem=w4_sem.at[0], recv_sem=w4_sem.at[1],
            device_id=sibling, device_id_type=MESH,
        )

    final = last_copy(core)
    final.start()

    sib_copy(0).wait_recv()
    node_grad = both(rep, yl)
    for k in range(1, YL):
        out_copy(k).wait_recv()
        node_grad += incoming[k].astype(jnp.float32)
    result_ref[...] = node_grad.astype(jnp.bfloat16)
    last_copy(1 - core).wait_recv()
    w_ref[...] = w_full[...]

    for copy in sib_sent + [w_copy, final] + y_sent:
        copy.wait_send()
    for k in range(1, YL):
        out_copy(k).wait_send()

    def drain(k, carry):
        pltpu.make_async_remote_copy(
            src_ref=w_half.at[(u + k) % PLANE], dst_ref=w_plane.at[k],
            send_sem=p1s_sem.at[k], recv_sem=p1r_sem.at[k], device_id=plane_peer(k), device_id_type=MESH,
        ).wait_send()
        spread(k, False).wait_send()
        return carry

    lax.fori_loop(1, PLANE, drain, 0)


def finish(grad_ref, w_ref, weight_ref, dx_ref, dw_ref):
    dx_ref[...] = lax.dot_general(
        grad_ref[...], weight_ref[...], (((1,), (1,)), ((), ())), preferred_element_type=jnp.float32
    ).astype(jnp.bfloat16)
    for half in range(2):
        for h in range(2):
            dw_ref[half * TILE:(half + 1) * TILE, h * TILE:(h + 1) * TILE] = (
                w_ref[half, h * 16:(h + 1) * 16].reshape(TILE, TILE)
            )


def shards(out_grad, node_input, weight, tile_vals, tile_rows, tile_cols, tile_count):
    vmem = pl.BlockSpec(memory_space=pltpu.VMEM)
    hbm = pl.BlockSpec(memory_space=pl.ANY)
    f32, bf16 = jnp.float32, jnp.bfloat16
    dma = pltpu.SemaphoreType.DMA
    slab = YL * CORES * ROWS
    node_grad, w_sum = pl.pallas_call(
        kernel,
        out_shape=(
            jax.ShapeDtypeStruct((ROWS, F), bf16),
            jax.ShapeDtypeStruct((2, PLANE, 8, TILE), f32),
        ),
        in_specs=[hbm] * 3 + [pl.BlockSpec(memory_space=pltpu.SMEM)] * 3,
        out_specs=(vmem, vmem),
        scratch_shapes=[
            pltpu.VMEM((PLANE * YH * UNITS, UNIT, F), bf16),
            pltpu.VMEM((CAP, TILE, TILE), bf16),
            pltpu.VMEM((CHAINS, SPAN + 1, TILE, F), f32),
            pltpu.VMEM((slab, F), bf16),
            pltpu.VMEM((slab, F), bf16),
            pltpu.VMEM((YL * CORES, ROWS, F), bf16),
            pltpu.VMEM((F, slab), bf16),
            pltpu.VMEM((YL, ROWS, F), bf16),
            pltpu.VMEM((YL, ROWS, F), bf16),
            pltpu.VMEM((YL, ROWS, F), bf16),
            pltpu.VMEM((2, PLANE, 8, TILE), f32),
            pltpu.VMEM((PLANE, 8, TILE), f32),
            pltpu.VMEM((PLANE, 8, TILE), f32),
            pltpu.VMEM((PLANE, 8, TILE), f32),
            pltpu.VMEM((Y, 8, TILE), f32),
            pltpu.VMEM((Y, 8, TILE), f32),
            pltpu.VMEM((2, PLANE, 8, TILE), f32),
            pltpu.SMEM((CAP,), jnp.int32),
            pltpu.SMEM((16 * CHAINS,), jnp.int32),
            dma((3,)),
            dma((len(EDGES),)), dma((len(EDGES),)),
            dma((1,)), dma((1,)),
            dma((2 * YL,)), dma((2 * YL,)),
            dma((YL,)), dma((YL,)),
            dma((YL,)), dma((YL,)),
            dma((2,)),
            dma((PLANE,)), dma((PLANE,)),
            dma((Y,)), dma((Y,)),
            dma((PLANE,)), dma((PLANE,)),
            dma((2,)),
        ],
        compiler_params=pltpu.CompilerParams(
            collective_id=0, has_side_effects=True, vmem_limit_bytes=60 * 1024 * 1024
        ),
        cost_estimate=pl.CostEstimate(flops=2_000_000_000, bytes_accessed=5_000_000, transcendentals=0),
    )(
        out_grad.reshape(UNITS, UNIT, F),
        node_input,
        tile_vals.reshape(CAP, TILE, TILE),
        tile_rows.reshape(1, CAP),
        tile_cols.reshape(1, CAP),
        tile_count.reshape(1, 1),
    )
    return pl.pallas_call(
        finish,
        out_shape=(
            jax.ShapeDtypeStruct((ROWS, F), bf16),
            jax.ShapeDtypeStruct((F, F), f32),
        ),
        in_specs=[vmem] * 3,
        out_specs=(vmem, vmem),
        compiler_params=pltpu.CompilerParams(vmem_limit_bytes=60 * 1024 * 1024),
    )(node_grad, w_sum, weight)


def solution(mesh):
    placed = (
        P(("rep", "row"), None),
        P(("row", "rep"), None),
        P(),
        P("row", "rep", None, None, None),
        P("row", "rep", None),
        P("row", "rep", None),
        P("row", "rep"),
    )
    return jax.shard_map(
        shards,
        mesh=mesh,
        in_specs=placed,
        out_specs=(P(("row", "rep"), None), P()),
        check_vma=False,
    )
```
